256 devices in a mesh: dp: 2 (over x_lo), ctx: 32 (over z, y), head: 4 (over x_hi, core).
Axes of the slice: x: 4 (x_hi: 2, x_lo: 2; x = x_hi * 2 + x_lo), y: 4, z: 8, core: 2. Of those that a mesh axis runs over, the one named last changes fastest.
Arguments:
- queries: bfloat16 [16384, 4096], P(('dp', 'ctx'), 'head'), parts along dimension 0, may hold values from -100 to 100
- keys: bfloat16 [16384, 1024], P(('dp', 'ctx'), 'head'), parts along dimension 0, may hold values from -13 to 13
- values: bfloat16 [16384, 1024], P(('dp', 'ctx'), 'head'), parts along dimension 0, may hold values from -6 to 6
- latents: bfloat16 [512, 4096], P(None, 'head'), may hold values from -400 to 400
- norm_gain: float32 [4096], P('head'), may hold values from 0.1 to 1.9
- block_doc: int32 [128], P('dp'), parts along dimension 0, may hold values from 0 to 15, as said below
- block_source: int32 [128], P('dp'), parts along dimension 0, may hold values from 0 to 63, as said below
Outputs:
- attended: bfloat16 [16384, 4096], P(('dp', 'ctx'), 'head'), parts along dimension 0
- embeddings: float32 [32, 4096], P('dp', 'head'), parts along dimension 0
The draws below stay inside these ranges and needn't reach their ends.
There are 2 independent parts, one for each index of `dp`. The reference program is written for one: setup_inputs(seed, part) draws one part's arguments, and reference() takes and returns one part's arrays. A program takes and returns all parts, laid end to end along the dimension named above; an argument that names none is the same for every part. Nothing has to cross between parts.
Inputs may be any that keep to these rules, and one draw needn't show every extreme that they name: `block_doc`: documents are whole runs of blocks in increasing id order; every document has one or more blocks and one has exactly 40. block_source is a permutation of the 64 blocks.
All inputs are finite; a program needn't handle non-finite values.
Results may differ from the reference program's by a relative error of at most 0.011.
Values may be sent and summed in bfloat16 or wider, within the bound.
A program may use at most 128 MiB of HBM per device.

```python
import math
import jax
import jax.numpy as jnp
from jax import lax

HEADS = 32
KV_HEADS = 8
HEAD_DIM = 128
LATENTS = 512
POOL_HEADS = 8
TOK_DEV = 256
BLOCK = 128
TOKENS = 8192
BLOCKS = 64
DOCS = 16
LONG_BLOCKS = 40


def key_rows(key):
    return jax.random.truncated_normal(key, -6.0, 6.0, (TOKENS, KV_HEADS * HEAD_DIM), jnp.float32)


def draw_keys(key, part):
    rows_out = key_rows(key)
    return rows_out.astype(jnp.bfloat16)


def draw_queries(key, part):
    key = jax.random.fold_in(key, 7)
    noise = 2.5 * jax.random.truncated_normal(key, -6.0, 6.0, (TOKENS, HEADS * HEAD_DIM), jnp.float32)
    return noise.astype(jnp.bfloat16)


def draw_latents(key, part):
    key = jax.random.fold_in(key, 11)
    base_rows = 1.5 * jax.random.truncated_normal(key, -6.0, 6.0, (LATENTS, HEADS * HEAD_DIM), jnp.float32)
    return base_rows.astype(jnp.bfloat16)


def doc_of_blocks(key):
    key = jax.random.fold_in(key, 13)
    remaining = BLOCKS - LONG_BLOCKS
    long_index = jax.random.randint(jax.random.fold_in(key, 1), (), 0, DOCS)
    shuffled = jax.random.permutation(jax.random.fold_in(key, 2), remaining - 1) + 1
    chosen = jnp.sort(shuffled[:DOCS - 2]).astype(jnp.int32)
    bounds = jnp.concatenate([jnp.zeros((1,), jnp.int32), chosen, jnp.full((1,), remaining, jnp.int32)])
    short_lengths = bounds[1:] - bounds[:-1]
    doc_index = jnp.arange(DOCS)
    short_index = jnp.clip(doc_index - (doc_index > long_index).astype(jnp.int32), 0, DOCS - 2)
    lengths = jnp.where(doc_index == long_index, LONG_BLOCKS, jnp.take(short_lengths, short_index))
    ends = jnp.cumsum(lengths)
    block_index = jnp.arange(BLOCKS)
    return jnp.sum((block_index[:, None] >= ends[None, :]).astype(jnp.int32), axis=1).astype(jnp.int32)


def draw_block_doc(key, part):
    shared = doc_of_blocks(key)
    return shared


def draw_block_source(key, part):
    doc_ids = doc_of_blocks(key)
    key = jax.random.fold_in(key, 17)
    doc_rank = jax.random.permutation(key, DOCS).astype(jnp.int32)
    block_index = jnp.arange(BLOCKS, dtype=jnp.int32)
    sort_scores = jnp.take(doc_rank, doc_ids) * BLOCKS + block_index
    listing = jnp.argsort(sort_scores, stable=True).astype(jnp.int32)
    per_shard = TOK_DEV // BLOCK
    shards = BLOCKS // per_shard
    shard_of = block_index // per_shard
    slot = block_index % per_shard
    return jnp.take(listing, slot * shards + shard_of).astype(jnp.int32)


def level_of(stream_key, extent, cuts, low, high):
    level = 1.0
    for axis_at, blocks in cuts:
        steps = jax.random.uniform(jax.random.fold_in(jax.random.fold_in(stream_key, 6), axis_at), (blocks,), jnp.float32, low / len(cuts), high / len(cuts))
        level = level * jnp.repeat(jnp.exp(steps), extent[axis_at] // blocks).reshape((-1,) + (1,) * (len(extent) - 1 - axis_at))
    return level


def normal_values(key, shape, spread, reach, cuts=(), kind=jnp.bfloat16):
    array = jax.random.normal(key, shape, jnp.float32) * spread
    if len(cuts) > 0:
        array = level_of(key, shape, cuts, -0.22, 0.18) * array
    return jnp.clip(array, min=-reach, max=reach).astype(kind)


def setup_inputs(seed: int = 0, part: int = 0) -> dict:
    key_list = jax.random.split(jax.random.key(seed), 8)
    part_keys = jax.random.split(jax.random.fold_in(key_list[7], part), 8)
    queries = draw_queries(jax.random.fold_in(jax.random.fold_in(key_list[7], part), 71), part)
    keys = draw_keys(jax.random.fold_in(jax.random.fold_in(key_list[7], part), 71), part)
    values = normal_values(part_keys[2], (TOKENS, KV_HEADS * HEAD_DIM), 1.0, 6.0, ((0, 32), (1, 4)))
    latents = draw_latents(jax.random.fold_in(key_list[7], 71), part)
    norm_gain = jnp.clip(1.0 + 0.18 * jax.random.normal(key_list[4], (HEADS * HEAD_DIM,), jnp.float32), 0.1, 1.9)
    block_doc = draw_block_doc(jax.random.fold_in(jax.random.fold_in(key_list[7], part), 71), part)
    block_source = draw_block_source(jax.random.fold_in(jax.random.fold_in(key_list[7], part), 71), part)
    return dict(queries=queries, keys=keys, values=values, latents=latents, norm_gain=norm_gain, block_doc=block_doc, block_source=block_source)


def reference(queries, keys, values, latents, norm_gain, block_doc, block_source):
    width = HEADS * HEAD_DIM
    group_size = HEADS // KV_HEADS
    score_scale = HEAD_DIM ** (-0.5)
    offsets = jnp.arange(BLOCK, dtype=jnp.int32)
    token_doc = jnp.repeat(block_doc, BLOCK)
    anchor = (block_source[:, None] * BLOCK + offsets[None, :]).reshape(-1).astype(jnp.int32)
    moved_queries = jnp.take(queries, anchor, axis=0)
    moved_doc = jnp.take(token_doc, anchor, axis=0)
    query_rows = math.gcd(TOKENS, 512)
    query_blocks = moved_queries.reshape(TOKENS // query_rows, query_rows, KV_HEADS, group_size, HEAD_DIM)
    doc_blocks = moved_doc.reshape(TOKENS // query_rows, query_rows)
    key_heads = keys.reshape(TOKENS, KV_HEADS, HEAD_DIM)
    value_heads = values.reshape(TOKENS, KV_HEADS, HEAD_DIM)

    def attend_block(pieces):
        query_block, doc_block = pieces
        same_doc = doc_block[:, None] == token_doc[None, :]

        def attend_head(kv_head):
            query_head = lax.dynamic_index_in_dim(query_block, kv_head, 1, keepdims=False).astype(jnp.float32)
            key_head = lax.dynamic_index_in_dim(key_heads, kv_head, 1, keepdims=False).astype(jnp.float32)
            value_head = lax.dynamic_index_in_dim(value_heads, kv_head, 1, keepdims=False).astype(jnp.float32)
            scores = jnp.einsum('qgd,kd->qgk', query_head, key_head) * score_scale
            scores = jnp.where(same_doc[:, None, :], scores, -jnp.inf)
            peak = lax.optimization_barrier(jnp.max(scores, axis=-1, keepdims=True))
            weights = jnp.exp(scores - peak)
            denominator = lax.optimization_barrier(jnp.sum(weights, axis=-1))
            rounded = lax.optimization_barrier(weights.astype(jnp.bfloat16)).astype(jnp.float32)
            mixed = jnp.einsum('qgk,kd->qgd', rounded, value_head)
            return mixed / denominator[:, :, None]
        per_head = lax.map(attend_head, jnp.arange(KV_HEADS, dtype=jnp.int32))
        return jnp.transpose(per_head, (1, 0, 2, 3)).reshape(query_rows, width).astype(jnp.bfloat16)
    attended = lax.map(attend_block, (query_blocks, doc_blocks)).reshape(TOKENS, width)
    as_float = attended.astype(jnp.float32)
    mean_square = lax.optimization_barrier(jnp.mean(as_float * as_float, axis=-1, keepdims=True))
    normed = (as_float * lax.rsqrt(mean_square + 1e-05) * norm_gain).astype(jnp.bfloat16)
    pool_width = width // POOL_HEADS
    one_hot = (moved_doc[:, None] == jnp.arange(DOCS, dtype=jnp.int32)[None, :]).astype(jnp.float32)
    doc_parts = []
    for pool_head in range(POOL_HEADS):
        normed_head = normed[:, pool_head * pool_width:(pool_head + 1) * pool_width]
        latent_head = latents[:, pool_head * pool_width:(pool_head + 1) * pool_width]
        scores = lax.dot_general(normed_head, latent_head, (((1,), (1,)), ((), ())), preferred_element_type=jnp.float32) * pool_width ** (-0.5)
        peak = lax.optimization_barrier(jnp.max(scores, axis=-1, keepdims=True))
        weights = jnp.exp(scores - peak)
        weights = weights / lax.optimization_barrier(jnp.sum(weights, axis=-1, keepdims=True))
        pooled = jnp.dot(weights.astype(jnp.bfloat16), latent_head, preferred_element_type=jnp.float32)
        doc_parts.append(lax.dot_general(one_hot, pooled, (((0,), (0,)), ((), ())), precision=lax.Precision.HIGHEST, preferred_element_type=jnp.float32))
    doc_sums = jnp.concatenate(doc_parts, axis=1)
    mean_doc = lax.optimization_barrier(jnp.mean(doc_sums * doc_sums, axis=-1, keepdims=True))
    embeddings = doc_sums * lax.rsqrt(mean_doc + 1e-05)
    return (attended, embeddings)
```

```python
import math

import jax
import jax.numpy as jnp
from jax import lax
from jax.experimental import pallas as pl
from jax.experimental.pallas import tpu as pltpu
from jax.sharding import PartitionSpec as P

HEADS = 32
HEAD_DIM = 128
BLOCK = 128
BLOCKS = 64
LONG = 40
DOCS = 16
CHANNELS = HEADS * HEAD_DIM
PIECE = 8
ROWS = 4 * PIECE
TILE = 256
CHUNK = 1024
LONG_KEYS = LONG * BLOCK
SHORT_KEYS = (BLOCKS - LONG) * BLOCK
EPS = 1e-05
MESH = pl.DeviceIdType.MESH
F32 = jnp.float32
BF16 = jnp.bfloat16


def loop(count, body):
    def step(i, carry):
        body(i)
        return carry

    lax.fori_loop(0, count, step, 0)


class Place:
    def __init__(self):
        self.ctx = lax.axis_index("ctx")
        head = lax.axis_index("head")
        self.z = self.ctx // 4
        self.y = self.ctx % 4
        self.plane = head // 2
        self.core = head % 2
        self.kv = self.z % 4
        self.piece = (self.z // 4) * 8 + self.y * 2 + self.core

    def at(self, z, y, core, plane=None):
        plane = self.plane if plane is None else plane
        return {"ctx": z * 4 + y, "head": plane * 2 + core}

    def worker(self, kv, piece):
        return (kv + 4 * (piece // 8), (piece % 8) // 2, piece % 2)

    def is_me(self, z, y, core):
        return (z == self.z) & (y == self.y) & (core == self.core)


def enter(me, others=0):
    barrier = pltpu.get_barrier_semaphore()

    def greet(i):
        z, y, core = i // 8, (i // 2) % 4, i % 2

        @pl.when(jnp.logical_not(me.is_me(z, y, core)))
        def _():
            pl.semaphore_signal(barrier, 1, device_id=me.at(z, y, core), device_id_type=MESH)

    loop(64, greet)
    if others:

        def greet_other(kv):
            pl.semaphore_signal(
                barrier,
                1,
                device_id=me.at(kv + 4 * (me.z // 4), me.y, me.core, 1 - me.plane),
                device_id_type=MESH,
            )

        loop(4, greet_other)
    pl.semaphore_wait(barrier, 63 + others)


def send(src, dst, send_sem, recv_sem, device):
    return pltpu.make_async_remote_copy(
        src_ref=src, dst_ref=dst, send_sem=send_sem, recv_sem=recv_sem, device_id=device, device_id_type=MESH
    )


def arrived(ref, sem):
    pltpu.make_async_copy(ref, ref, sem).wait()


def spread_kernel(
    q_ref, k_ref, v_ref, lat_ref, gain_ref,
    qp_ref, kv_ref, lat_out, gain_out,
    qs, s_a, r_a, s_b, r_b, s_c, r_c, s_s, r_s, s_q, r_q, s_l, r_l,
):
    me = Place()
    z, y, core = me.z, me.y, me.core
    enter(me)
    up, down = (y + 1) % 4, (y + 3) % 4
    mine = me.kv // 2 == core

    def column(run):
        for half in range(2):
            for far in range(2):
                for kind in range(2):
                    to_z = 2 * core + half + 4 * far
                    slot = half * 4 + far * 2 + kind
                    src = (k_ref, v_ref)[kind].at[:, pl.ds(half * HEAD_DIM, HEAD_DIM)]
                    dst = kv_ref.at[kind, pl.ds(me.ctx * 256, 256), :]
                    here = (to_z == z) & (core == kind)
                    copy = send(src, dst, s_a.at[slot], r_a.at[z], me.at(to_z, y, kind))
                    run(here, copy, src, dst)

    def start_column(here, copy, src, dst):
        @pl.when(here)
        def _():
            pltpu.make_async_copy(src, dst, r_a.at[z]).start()

        @pl.when(jnp.logical_not(here))
        def _():
            copy.start()

    def end_column(here, copy, src, dst):
        @pl.when(jnp.logical_not(here))
        def _():
            copy.wait_send()

    column(start_column)

    def pool_inputs():
        other = me.at(z, y, 1 - core)
        half = me.kv % 2
        lat = lat_ref.at[:, pl.ds(pl.multiple_of(half * 512, 512), 512)]
        gain = gain_ref.at[half]
        return (
            pltpu.make_async_copy(lat, lat_out, r_l.at[0]),
            pltpu.make_async_copy(gain, gain_out, r_l.at[1]),
            send(lat, lat_out, s_l.at[0], r_l.at[0], other),
            send(gain, gain_out, s_l.at[1], r_l.at[1], other),
        )

    @pl.when(mine)
    def _():
        for copy in pool_inputs():
            copy.start()

    for half in range(2):
        for block in range(2):
            for pair in range(8):
                tile = q_ref[block * BLOCK + pair * 16 : block * BLOCK + pair * 16 + 16, half * 512 : half * 512 + 512]
                tile = tile.astype(F32)
                for part in range(2):
                    rows = tile[part * 8 : part * 8 + 8]
                    rows = jnp.concatenate([rows[:, h * 128 : h * 128 + 128] for h in range(4)], axis=0)
                    qs[half * 16 + pair * 2 + part, block * ROWS : block * ROWS + ROWS, :] = rows.astype(BF16)

    def query(j, run):
        i = (j + me.ctx) % 32
        to = me.worker(2 * core + i // 16, i % 16)
        run(
            me.is_me(*to),
            send(qs.at[i], qp_ref.at[me.ctx], s_q.at[i], r_q.at[me.ctx], me.at(*to)),
            pltpu.make_async_copy(qs.at[i], qp_ref.at[me.ctx], r_q.at[me.ctx]),
        )

    def start_query(here, remote, local):
        @pl.when(here)
        def _():
            local.start()

        @pl.when(jnp.logical_not(here))
        def _():
            remote.start()

    def end_query(here, remote, local):
        @pl.when(jnp.logical_not(here))
        def _():
            remote.wait_send()

    loop(32, lambda j: query(j, start_query))

    def rows_of(from_z, from_y, first=0, count=256):
        start = pl.multiple_of((from_z * 4 + from_y) * 256 + first, 128)
        return kv_ref.at[core, pl.ds(start, count), :]

    def to_core(from_z, from_y):
        s = from_z * 4 + from_y
        rows = rows_of(from_z, from_y)
        return send(rows, rows, s_s.at[s], r_s.at[s], me.at(z, y, 1 - core))

    def near(from_z):
        rows = rows_of(from_z, y)
        return (
            send(rows, rows, s_b.at[0, from_z], r_b.at[0, from_z], me.at(z, up, core)),
            send(rows, rows, s_b.at[1, from_z], r_b.at[1, from_z], me.at(z, down, core)),
            to_core(from_z, y),
        )

    def onward(from_z):
        one = rows_of(from_z, down, 0, 128)
        two = rows_of(from_z, up, 128, 128)
        return (
            send(one, one, s_c.at[0, from_z], r_c.at[0, from_z], me.at(z, up, core)),
            to_core(from_z, down),
            send(two, two, s_c.at[1, from_z], r_c.at[1, from_z], me.at(z, down, core)),
            to_core(from_z, up),
        )

    def order(j):
        odd = j % 2
        return (z + odd * ((j + 1) // 2) + (1 - odd) * (8 - j // 2)) % 8

    def ring(j):
        @pl.when(j < 8)
        def _():
            from_z = order(j)
            arrived(rows_of(from_z, y), r_a.at[from_z])
            for copy in near(from_z):
                copy.start()

        @pl.when((j >= 2) & (j < 10))
        def _():
            from_z = order(j - 2)
            copies = onward(from_z)
            arrived(rows_of(from_z, down), r_b.at[0, from_z])
            copies[0].start()
            copies[1].start()
            arrived(rows_of(from_z, up), r_b.at[1, from_z])
            copies[2].start()
            copies[3].start()

        @pl.when(j >= 4)
        def _():
            from_z = order(j - 4)
            opposite = (y + 2) % 4
            arrived(rows_of(from_z, opposite, 0, 128), r_c.at[0, from_z])
            arrived(rows_of(from_z, opposite, 128, 128), r_c.at[1, from_z])
            to_core(from_z, opposite).start()

    loop(12, ring)

    def finish_ring(from_z):
        for copy in near(from_z) + onward(from_z) + (to_core(from_z, (y + 2) % 4),):
            copy.wait_send()

    column(end_column)
    loop(8, finish_ring)
    loop(32, lambda j: query(j, end_query))

    def finish(s):
        arrived(qp_ref.at[s], r_q.at[s])
        arrived(kv_ref.at[1 - core, pl.ds(pl.multiple_of(s * 256, 256), 256), :], r_s.at[s])

    loop(32, finish)
    for copy in pool_inputs()[:2]:
        copy.wait()

    @pl.when(mine)
    def _():
        for copy in pool_inputs()[2:]:
            copy.wait_send()


def spread(queries, keys, values, latents, gain):
    dma = pltpu.SemaphoreType.DMA
    hbm = pl.BlockSpec(memory_space=pl.ANY)
    vmem = pl.BlockSpec(memory_space=pltpu.VMEM)
    return pl.pallas_call(
        spread_kernel,
        out_shape=(
            jax.ShapeDtypeStruct((32, 2 * ROWS, HEAD_DIM), BF16),
            jax.ShapeDtypeStruct((2, BLOCKS * BLOCK, HEAD_DIM), BF16),
            jax.ShapeDtypeStruct((512, 512), BF16),
            jax.ShapeDtypeStruct((4, 128), F32),
        ),
        in_specs=[vmem, hbm, hbm, hbm, hbm],
        out_specs=(hbm, hbm, hbm, hbm),
        scratch_shapes=[
            pltpu.VMEM((32, 2 * ROWS, HEAD_DIM), BF16),
            dma((8,)), dma((8,)),
            dma((2, 8)), dma((2, 8)),
            dma((2, 8)), dma((2, 8)),
            dma((32,)), dma((32,)),
            dma((32,)), dma((32,)),
            dma((2,)), dma((2,)),
        ],
        compiler_params=pltpu.CompilerParams(
            collective_id=0, has_side_effects=True, vmem_limit_bytes=32 * 1024 * 1024
        ),
        name="spread",
    )(queries, keys, values, latents, gain)


def attend_kernel(doc_ref, source_ref, q_ref, kv_ref, out_ref, sq_ref, hot_ref, ka, va, qa, scores, peak, o_ref):
    first = lax.fori_loop(
        0,
        BLOCKS - LONG + 1,
        lambda i, found: jnp.where(doc_ref[i] == doc_ref[i + LONG - 1], i, found),
        jnp.int32(0),
    )

    def packed(i):
        return jnp.where(i < LONG, first + i, jnp.where(i - LONG < first, i - LONG, i))

    scale = math.log2(math.e) * HEAD_DIM ** (-0.5)

    def arrange(i):
        at = packed(i)
        here = pl.ds(pl.multiple_of(i * BLOCK, BLOCK), BLOCK)
        there = pl.ds(pl.multiple_of(at * BLOCK, BLOCK), BLOCK)
        key = kv_ref[0, there, :]
        ka[here, 0:128] = key
        ka[here, 128:256] = key
        va[here, 0:128] = kv_ref[1, there, :]
        va[here, 128:256] = jnp.ones((BLOCK, 128), BF16)
        query = q_ref[pl.ds(pl.multiple_of(at * ROWS, ROWS), ROWS), :].astype(F32) * scale
        high = query.astype(BF16)
        rows = pl.ds(pl.multiple_of(i * ROWS, ROWS), ROWS)
        qa[rows, 0:128] = high
        qa[rows, 128:256] = (query - high.astype(F32)).astype(BF16)

    loop(BLOCKS, arrange)

    def tile_rows(t):
        return pl.ds(pl.multiple_of(t * TILE, TILE), TILE)

    def score_chunk(t, slot, c, base, top, docs=None):
        q = qa[tile_rows(t), :]
        k = ka[base + c * CHUNK : base + (c + 1) * CHUNK, :]
        s = lax.dot_general(q, k, (((1,), (1,)), ((), ())), preferred_element_type=F32)
        if docs is not None:
            parts = []
            for b in range(CHUNK // BLOCK):
                key_doc = doc_ref[packed(jnp.int32((base + c * CHUNK) // BLOCK + b))]
                parts.append(jnp.where(docs == key_doc, s[:, b * 128 : b * 128 + 128], -1e30))
            s = jnp.concatenate(parts, axis=1)
        scores[slot, :, c * CHUNK : (c + 1) * CHUNK] = s
        for b in range(CHUNK // 128):
            part = s[:, b * 128 : b * 128 + 128]
            top = part if top is None else jnp.maximum(top, part)
        return top

    def close_scores(slot, top):
        peak[slot] = jnp.broadcast_to(jnp.max(top, axis=1, keepdims=True), (TILE, 128))

    def mix_chunk(slot, c, base, total):
        m = peak[slot]
        parts = []
        for b in range(CHUNK // 128):
            s = scores[slot, :, c * CHUNK + b * 128 : c * CHUNK + b * 128 + 128]
            parts.append(jnp.exp2(s - m).astype(BF16))
        w = jnp.concatenate(parts, axis=1)
        v = va[base + c * CHUNK : base + (c + 1) * CHUNK, :]
        add = jnp.dot(w, v, preferred_element_type=F32)
        return add if total is None else total + add

    def close_mix(t, total):
        o_ref[tile_rows(t), :] = (total[:, 0:128] / total[:, 128:256]).astype(BF16)

    long_tiles = LONG * ROWS // TILE
    long_chunks = LONG_KEYS // CHUNK
    short_tiles = (BLOCKS - LONG) * ROWS // TILE
    short_chunks = SHORT_KEYS // CHUNK

    top = None
    for c in range(long_chunks):
        top = score_chunk(0, 0, c, 0, top)
    close_scores(0, top)

    def step(t):
        slot = t % 2
        top, total = None, None
        for c in range(long_chunks):
            top = score_chunk(t + 1, 1 - slot, c, 0, top)
            total = mix_chunk(slot, c, 0, total)
        close_scores(1 - slot, top)
        close_mix(t, total)

    loop(long_tiles - 1, step)

    def row_docs(t):
        per = TILE // ROWS
        return jnp.concatenate(
            [jnp.full((ROWS, 128), doc_ref[packed(t * per + b)], jnp.int32) for b in range(per)], axis=0
        )

    def short_step(i):
        t = long_tiles + i
        slot = t % 2
        docs = row_docs(t)
        top, total = None, None
        for c in range(short_chunks):
            top = score_chunk(t, slot, c, LONG_KEYS, top, docs)
        close_scores(slot, top)
        for c in range(short_chunks):
            total = mix_chunk(slot, c, LONG_KEYS, total)
        close_mix(t, total)

    last = long_tiles - 1
    total = None
    for c in range(long_chunks):
        total = mix_chunk(last % 2, c, 0, total)
    close_mix(last, total)
    loop(short_tiles, short_step)

    lanes = lax.broadcasted_iota(jnp.int32, (PIECE, 128), 1)

    def squares(half):
        part = peak[0]
        high = part.astype(BF16)
        low = (part - high.astype(F32)).astype(BF16)
        ones = jnp.ones((8, 128), BF16)
        dims = (((1,), (1,)), ((), ()))
        sq_ref[:, half * 256 : half * 256 + 256] = lax.dot_general(
            ones, high, dims, preferred_element_type=F32
        ) + lax.dot_general(ones, low, dims, preferred_element_type=F32)
        hot_ref[:, half * 256 : half * 256 + 256] = jnp.transpose(scores[0, :, 0:128])[0:DOCS].astype(BF16)

    for half in range(2):
        def move_half(i, half=half):
            p = half * 32 + i
            at = source_ref[p]
            doc = doc_ref[at]
            row = jnp.where(at < first, at + LONG, jnp.where(at < first + LONG, at - first, at))
            piece = o_ref[pl.ds(pl.multiple_of(row * ROWS, ROWS), ROWS), :]
            out_ref[p] = piece
            wide = piece.astype(F32)
            wide = wide * wide
            here = pl.ds(pl.multiple_of(i * PIECE, PIECE), PIECE)
            peak[0, here, :] = wide[0:8] + wide[8:16] + wide[16:24] + wide[24:32]
            scores[0, here, 0:128] = (lanes == doc).astype(F32)

        loop(32, move_half)
        squares(half)


def attend(block_doc, block_source, q, kv):
    smem = pl.BlockSpec(memory_space=pltpu.SMEM)
    vmem = pl.BlockSpec(memory_space=pltpu.VMEM)
    return pl.pallas_call(
        attend_kernel,
        out_shape=(
            jax.ShapeDtypeStruct((BLOCKS, ROWS, HEAD_DIM), BF16),
            jax.ShapeDtypeStruct((8, BLOCKS * PIECE), F32),
            jax.ShapeDtypeStruct((DOCS, BLOCKS * PIECE), BF16),
        ),
        in_specs=[smem, smem, vmem, vmem],
        out_specs=(vmem, vmem, vmem),
        scratch_shapes=[
            pltpu.VMEM((BLOCKS * BLOCK, 256), BF16),
            pltpu.VMEM((BLOCKS * BLOCK, 256), BF16),
            pltpu.VMEM((BLOCKS * ROWS, 256), BF16),
            pltpu.VMEM((2, TILE, LONG_KEYS), F32),
            pltpu.VMEM((2, TILE, 128), F32),
            pltpu.VMEM((BLOCKS * ROWS, HEAD_DIM), BF16),
        ],
        compiler_params=pltpu.CompilerParams(vmem_limit_bytes=48 * 1024 * 1024),
        name="attend",
    )(block_doc, block_source, q, kv)


def collect_kernel(
    o_ref, sq_ref, hot_ref, lat_ref, gain_ref,
    att_ref, emb_ref,
    home, sq_in, doc_out, doc_in, norm_out, norm_in, row_out, row_in,
    s_o, r_o, s_sq, r_sq, s_d, r_d, s_n, r_n, s_e, r_e,
):
    me = Place()
    enter(me, 4)
    me8 = me.plane * 4 + me.kv
    to_core = me.kv // 2
    half = me.kv % 2

    def partners(src, box, s_sem, r_sem, run):
        def one(i):
            @pl.when(i != me8)
            def _():
                device = me.at(i % 4 + 4 * (me.z // 4), me.y, me.core, i // 4)
                run(send(src, box.at[me8], s_sem.at[i], r_sem.at[me8], device))

        loop(8, one)

    def from_partners(box, r_sem):
        def one(i):
            @pl.when(i != me8)
            def _():
                arrived(box.at[i], r_sem.at[i])

        loop(8, one)

    start = lambda copy: copy.start()
    sent = lambda copy: copy.wait_send()

    partners(sq_ref, sq_in, s_sq, r_sq, start)
    sq_in[me8] = sq_ref[...]

    def result(j, run):
        s = (j + me.ctx) % 32
        src = o_ref.at[pl.ds(2 * s, 2)]
        slot = half * 16 + me.piece
        run(
            me.is_me(s // 4, s % 4, to_core),
            send(src, home.at[slot], s_o.at[s], r_o.at[slot], me.at(s // 4, s % 4, to_core)),
            pltpu.make_async_copy(src, home.at[slot], r_o.at[slot]),
        )

    def start_either(here, remote, local):
        @pl.when(here)
        def _():
            local.start()

        @pl.when(jnp.logical_not(here))
        def _():
            remote.start()

    def end_either(here, remote, local):
        @pl.when(jnp.logical_not(here))
        def _():
            remote.wait_send()

    loop(32, lambda j: result(j, start_either))

    from_partners(sq_in, r_sq)
    channel_total = jnp.sum(sq_in[...], axis=0)[0:1]
    factor = lax.rsqrt(channel_total / CHANNELS + EPS)
    factor = jnp.transpose(jnp.broadcast_to(factor, (128, BLOCKS * PIECE)))
    whole = o_ref[...].astype(F32).reshape(BLOCKS, 4, PIECE, 128)
    normed = []
    for h in range(4):
        part = whole[:, h].reshape(BLOCKS * PIECE, 128)
        normed.append((part * factor * gain_ref[h : h + 1, :]).astype(BF16))
    normed = jnp.concatenate(normed, axis=1)

    lat = lat_ref[...]
    s = lax.dot_general(normed, lat, (((1,), (1,)), ((), ())), preferred_element_type=F32) * 512 ** (-0.5)
    w = jnp.exp(s - jnp.max(s, axis=-1, keepdims=True))
    w = (w / jnp.sum(w, axis=-1, keepdims=True)).astype(BF16)
    by_doc = jnp.dot(hot_ref[...], w, preferred_element_type=F32)
    sums = None
    for _ in range(3):
        part = by_doc.astype(BF16)
        by_doc = by_doc - part.astype(F32)
        add = jnp.dot(part, lat, preferred_element_type=F32)
        sums = add if sums is None else sums + add

    doc_out[...] = jnp.zeros_like(doc_out)
    for h in range(4):
        doc_out[:, h, :] = sums[:, h * 128 : h * 128 + 128]

    def document(d, run):
        to = me.worker(me.kv, d)
        run(
            d == me.piece,
            send(doc_out.at[d], doc_in.at[me.piece], s_d.at[d], r_d.at[me.piece], me.at(*to)),
            pltpu.make_async_copy(doc_out.at[d], doc_in.at[me.piece], r_d.at[me.piece]),
        )

    loop(DOCS, lambda d: document(d, start_either))
    loop(DOCS, lambda d: arrived(doc_in.at[d], r_d.at[d]))
    total = jnp.sum(doc_in[...], axis=0)
    norm_out[...] = jnp.broadcast_to(jnp.sum(total * total, keepdims=True), (8, 128))
    partners(norm_out, norm_in, s_n, r_n, start)
    norm_in[me8] = norm_out[...]
    from_partners(norm_in, r_n)
    doc_total = jnp.sum(norm_in[...], axis=0)
    row_out[...] = total * lax.rsqrt(doc_total / CHANNELS + EPS)

    def share(j, run):
        s = (j + me.ctx) % 32
        dst = row_in.at[half, me.piece]
        slot = half * 16 + me.piece
        run(
            me.is_me(s // 4, s % 4, to_core),
            send(row_out, dst, s_e.at[s], r_e.at[slot], me.at(s // 4, s % 4, to_core)),
            pltpu.make_async_copy(row_out, dst, r_e.at[slot]),
        )

    loop(32, lambda j: share(j, start_either))

    loop(32, lambda i: arrived(home.at[i], r_o.at[i]))
    for side in range(2):
        for block in range(2):
            for pair in range(8):
                rows = []
                for part in range(2):
                    piece = home[side * 16 + pair * 2 + part, block].astype(F32)
                    rows.append(jnp.concatenate([piece[h * 8 : h * 8 + 8] for h in range(4)], axis=1))
                at = block * BLOCK + pair * 16
                att_ref[at : at + 16, side * 512 : side * 512 + 512] = jnp.concatenate(rows, axis=0).astype(BF16)

    loop(32, lambda i: arrived(row_in.at[i // 16, i % 16], r_e.at[i]))
    for side in range(2):
        for h in range(4):
            at = side * 512 + h * 128
            emb_ref[:, at : at + 128] = row_in[side, :, h, :]

    partners(sq_ref, sq_in, s_sq, r_sq, sent)
    partners(norm_out, norm_in, s_n, r_n, sent)
    loop(32, lambda j: result(j, end_either))
    loop(DOCS, lambda d: document(d, end_either))
    loop(32, lambda j: share(j, end_either))


def collect(results, squares, hot, latents, gain):
    dma = pltpu.SemaphoreType.DMA
    vmem = pl.BlockSpec(memory_space=pltpu.VMEM)
    return pl.pallas_call(
        collect_kernel,
        out_shape=(
            jax.ShapeDtypeStruct((256, 1024), BF16),
            jax.ShapeDtypeStruct((DOCS, 1024), F32),
        ),
        in_specs=[vmem] * 5,
        out_specs=(vmem, vmem),
        scratch_shapes=[
            pltpu.VMEM((32, 2, ROWS, HEAD_DIM), BF16),
            pltpu.VMEM((8, 8, BLOCKS * PIECE), F32),
            pltpu.VMEM((DOCS, 8, 128), F32),
            pltpu.VMEM((DOCS, 8, 128), F32),
            pltpu.VMEM((8, 128), F32),
            pltpu.VMEM((8, 8, 128), F32),
            pltpu.VMEM((8, 128), F32),
            pltpu.VMEM((2, DOCS, 8, 128), F32),
            dma((32,)), dma((32,)),
            dma((8,)), dma((8,)),
            dma((DOCS,)), dma((DOCS,)),
            dma((8,)), dma((8,)),
            dma((32,)), dma((32,)),
        ],
        compiler_params=pltpu.CompilerParams(
            collective_id=1, has_side_effects=True, vmem_limit_bytes=40 * 1024 * 1024
        ),
        name="collect",
    )(results, squares, hot, latents, gain)


def shards(queries, keys, values, latents, norm_gain, block_doc, block_source):
    q, kv, lat, gain = spread(queries, keys, values, latents, norm_gain.reshape(2, 4, 128))
    results, squares, hot = attend(block_doc, block_source, q.reshape(BLOCKS * ROWS, HEAD_DIM), kv)
    return collect(results, squares, hot, lat, gain)


def solution(mesh):
    in_specs = (
        P(("dp", "ctx"), "head"),
        P(("dp", "ctx"), "head"),
        P(("dp", "ctx"), "head"),
        P(None, "head"),
        P("head"),
        P("dp"),
        P("dp"),
    )
    out_specs = (P(("dp", "ctx"), "head"), P("dp", "head"))
    return jax.shard_map(shards, mesh=mesh, in_specs=in_specs, out_specs=out_specs, check_vma=False)
```

```python
import functools
import math

import jax
import jax.numpy as jnp
from jax import lax
from jax.experimental import pallas as pl
from jax.experimental.pallas import tpu as pltpu
from jax.sharding import PartitionSpec as P

HEADS = 32
HEAD_DIM = 128
BLOCK = 128
BLOCKS = 64
LONG = 40
DOCS = 16
CHANNELS = HEADS * HEAD_DIM
PIECE = 8
ROWS = 4 * PIECE
TILE = 640
SHORT_TILE = 384
CHUNK = 256
LONG_KEYS = LONG * BLOCK
SHORT_KEYS = (BLOCKS - LONG) * BLOCK
EPS = 1e-05
PARTS = 1
PART = 256 // PARTS
HALF = PART // 2
AHEAD = 4
Q_START = 4
Q_STEP = 4
LAG = 4
MESH = pl.DeviceIdType.MESH
F32 = jnp.float32
BF16 = jnp.bfloat16


def loop(count, body):
    def step(i, carry):
        body(i)
        return carry

    lax.fori_loop(0, count, step, 0)


class Place:
    def __init__(self):
        self.ctx = lax.axis_index("ctx")
        head = lax.axis_index("head")
        self.z = self.ctx // 4
        self.y = self.ctx % 4
        self.plane = head // 2
        self.core = head % 2
        self.kv = self.z % 4
        self.piece = (self.z // 4) * 8 + self.y * 2 + self.core

    def at(self, z, y, core, plane=None):
        plane = self.plane if plane is None else plane
        return {"ctx": z * 4 + y, "head": plane * 2 + core}

    def worker(self, kv, piece):
        return (kv + 4 * (piece // 8), (piece % 8) // 2, piece % 2)

    def is_me(self, z, y, core):
        return (z == self.z) & (y == self.y) & (core == self.core)


def enter(me, others=0):
    barrier = pltpu.get_barrier_semaphore()

    def greet(i):
        z, y, core = i // 8, (i // 2) % 4, i % 2

        @pl.when(jnp.logical_not(me.is_me(z, y, core)))
        def _():
            pl.semaphore_signal(barrier, 1, device_id=me.at(z, y, core), device_id_type=MESH)

    loop(64, greet)
    if others:

        def greet_other(i):
            here = i == 4
            z = jnp.where(here, me.z, i % 4 + 4 * (me.z // 4))
            core = jnp.where(here, 1 - me.core, me.core)
            pl.semaphore_signal(
                barrier, 1, device_id=me.at(z, me.y, core, 1 - me.plane), device_id_type=MESH
            )

        loop(others, greet_other)
    pl.semaphore_wait(barrier, 63 + others)


def send(src, dst, send_sem, recv_sem, device):
    return pltpu.make_async_remote_copy(
        src_ref=src, dst_ref=dst, send_sem=send_sem, recv_sem=recv_sem, device_id=device, device_id_type=MESH
    )


def arrived(ref, sem):
    pltpu.make_async_copy(ref, ref, sem).wait()


def start_either(here, remote, local):
    @pl.when(here)
    def _():
        local.start()

    @pl.when(jnp.logical_not(here))
    def _():
        remote.start()


def end_either(here, remote, local):
    @pl.when(jnp.logical_not(here))
    def _():
        remote.wait_send()


def spread_kernel(
    q_ref, k_ref, v_ref, lat_ref, gain_ref,
    qp_ref, kv_ref, lat_out, gain_out,
    q_in, qs, s_a, r_a, s_b, r_b, s_c, r_c, s_s, r_s, s_q, r_q, s_l, r_l, l_q,
):
    me = Place()
    z, y, core = me.z, me.y, me.core
    load_q = pltpu.make_async_copy(q_ref, q_in, l_q)
    load_q.start()
    enter(me)
    up, down = (y + 1) % 4, (y + 3) % 4
    mine = me.kv // 2 == core

    def order(j):
        odd = j % 2
        return odd * ((j + 1) // 2) + (1 - odd) * (8 - j // 2)

    def column(j, run):
        to_z = (z + order(j)) % 8

        @pl.when((to_z % 4) // 2 == core)
        def _():
            half = to_z % 2
            for part in range(PARTS):
                for kind in range(2):
                    first = part * PART
                    columns = pl.ds(pl.multiple_of(half * HEAD_DIM, HEAD_DIM), HEAD_DIM)
                    src = (k_ref, v_ref)[kind].at[pl.ds(first, PART), columns]
                    dst = kv_ref.at[kind, pl.ds(pl.multiple_of(me.ctx * 256 + first, PART), PART), :]
                    sem = r_a.at[part, z]
                    here = (to_z == z) & (core == kind)
                    copy = send(src, dst, s_a.at[part, kind, to_z], sem, me.at(to_z, y, kind))
                    run(here, copy, pltpu.make_async_copy(src, dst, sem))

    loop(AHEAD, lambda j: column(j, start_either))

    load_q.wait()

    def regroup(i):
        half, pair = i // 8, i % 8
        rows_at = pl.ds(pl.multiple_of(pair * 16, 16), 16)
        for block in range(2):
            tile = q_in[block, rows_at, pl.ds(pl.multiple_of(half * 512, 512), 512)].astype(F32)
            for part in range(2):
                rows = tile[part * 8 : part * 8 + 8]
                rows = jnp.concatenate([rows[:, h * 128 : h * 128 + 128] for h in range(4)], axis=0)
                qs[2 * i + part, block * ROWS : block * ROWS + ROWS, :] = rows.astype(BF16)

    loop(16, regroup)

    def query(j, run):
        i = (j + me.ctx) % 32
        to = me.worker(2 * core + i // 16, i % 16)
        run(
            me.is_me(*to),
            send(qs.at[i], qp_ref.at[me.ctx], s_q.at[i], r_q.at[me.ctx], me.at(*to)),
            pltpu.make_async_copy(qs.at[i], qp_ref.at[me.ctx], r_q.at[me.ctx]),
        )

    def rows_of(from_z, from_y, first=0, count=256):
        start = pl.multiple_of((from_z * 4 + from_y) * 256 + first, HALF)
        return kv_ref.at[core, pl.ds(start, count), :]

    def to_core(from_z):
        rows = kv_ref.at[core, pl.ds(pl.multiple_of(from_z * 1024, 1024), 1024), :]
        return send(rows, rows, s_s.at[from_z], r_s.at[from_z], me.at(z, y, 1 - core))

    def near(from_z, part):
        rows = rows_of(from_z, y, part * PART, PART)
        return (
            send(rows, rows, s_b.at[0, part, from_z], r_b.at[0, part, from_z], me.at(z, up, core)),
            send(rows, rows, s_b.at[1, part, from_z], r_b.at[1, part, from_z], me.at(z, down, core)),
        )

    def onward(from_z, part):
        one = rows_of(from_z, down, part * PART, HALF)
        two = rows_of(from_z, up, part * PART + HALF, HALF)
        return (
            send(one, one, s_c.at[0, part, from_z], r_c.at[0, part, from_z], me.at(z, up, core)),
            send(two, two, s_c.at[1, part, from_z], r_c.at[1, part, from_z], me.at(z, down, core)),
        )

    steps = 8 * PARTS

    def at_step(e):
        return (z + order(e // PARTS)) % 8, e % PARTS

    def ring(e):
        @pl.when(e < steps)
        def _():
            @pl.when((e % PARTS == 0) & (e // PARTS + AHEAD < 8))
            def _():
                column(e // PARTS + AHEAD, start_either)

            from_z, part = at_step(e)
            arrived(rows_of(from_z, y, part * PART, PART), r_a.at[part, from_z])
            for copy in near(from_z, part):
                copy.start()

        @pl.when((e >= Q_START) & (e < Q_START + 32 // Q_STEP))
        def _():
            for i in range(Q_STEP):
                query((e - Q_START) * Q_STEP + i, start_either)

        @pl.when((e >= LAG) & (e < steps + LAG))
        def _():
            from_z, part = at_step(e - LAG)
            copies = onward(from_z, part)
            arrived(rows_of(from_z, down, part * PART, PART), r_b.at[0, part, from_z])
            copies[0].start()
            arrived(rows_of(from_z, up, part * PART, PART), r_b.at[1, part, from_z])
            copies[1].start()

        @pl.when(e >= 2 * LAG)
        def _():
            from_z, part = at_step(e - 2 * LAG)
            opposite = (y + 2) % 4
            arrived(rows_of(from_z, opposite, part * PART, HALF), r_c.at[0, part, from_z])
            arrived(rows_of(from_z, opposite, part * PART + HALF, HALF), r_c.at[1, part, from_z])

            @pl.when(part == PARTS - 1)
            def _():
                to_core(from_z).start()

    loop(steps + 2 * LAG, ring)

    def pool_inputs():
        other = me.at(z, y, 1 - core)
        half = me.kv % 2
        lat = lat_ref.at[:, pl.ds(pl.multiple_of(half * 512, 512), 512)]
        gain = gain_ref.at[half]
        return (
            pltpu.make_async_copy(lat, lat_out, r_l.at[0]),
            pltpu.make_async_copy(gain, gain_out, r_l.at[1]),
            send(lat, lat_out, s_l.at[0], r_l.at[0], other),
            send(gain, gain_out, s_l.at[1], r_l.at[1], other),
        )

    @pl.when(mine)
    def _():
        for copy in pool_inputs():
            copy.start()

    loop(8, lambda j: column(j, end_either))

    def finish_ring(e):
        from_z, part = at_step(e)
        for copy in near(from_z, part) + onward(from_z, part):
            copy.wait_send()

    loop(steps, finish_ring)
    loop(32, lambda j: query(j, end_either))
    loop(32, lambda s: arrived(qp_ref.at[s], r_q.at[s]))

    def finish_core(from_z):
        to_core(from_z).wait_send()
        arrived(kv_ref.at[1 - core, pl.ds(pl.multiple_of(from_z * 1024, 1024), 1024), :], r_s.at[from_z])

    loop(8, finish_core)
    for copy in pool_inputs()[:2]:
        copy.wait()

    @pl.when(mine)
    def _():
        for copy in pool_inputs()[2:]:
            copy.wait_send()


def spread(queries, keys, values, latents, gain):
    dma = pltpu.SemaphoreType.DMA
    hbm = pl.BlockSpec(memory_space=pltpu.HBM)
    vmem = pl.BlockSpec(memory_space=pltpu.VMEM)
    return pl.pallas_call(
        spread_kernel,
        out_shape=(
            jax.ShapeDtypeStruct((32, 2 * ROWS, HEAD_DIM), BF16),
            jax.ShapeDtypeStruct((2, BLOCKS * BLOCK, HEAD_DIM), BF16),
            jax.ShapeDtypeStruct((512, 512), BF16),
            jax.ShapeDtypeStruct((4, 128), F32),
        ),
        in_specs=[hbm] * 5,
        out_specs=(vmem,) * 4,
        scratch_shapes=[
            pltpu.VMEM((2, BLOCK, 1024), BF16),
            pltpu.VMEM((32, 2 * ROWS, HEAD_DIM), BF16),
            dma((PARTS, 2, 8)), dma((PARTS, 8)),
            dma((2, PARTS, 8)), dma((2, PARTS, 8)),
            dma((2, PARTS, 8)), dma((2, PARTS, 8)),
            dma((8,)), dma((8,)),
            dma((32,)), dma((32,)),
            dma((2,)), dma((2,)),
            dma,
        ],
        compiler_params=pltpu.CompilerParams(
            collective_id=0, has_side_effects=True, vmem_limit_bytes=32 * 1024 * 1024
        ),
        name="spread",
    )(queries.reshape(2, BLOCK, 1024), keys, values, latents, gain)


def attend_kernel(doc_ref, source_ref, q_ref, kv_ref, out_ref, sq_ref, hot_ref, ka, va, qa, sq, hot, o_ref):
    first = lax.fori_loop(
        0,
        BLOCKS - LONG + 1,
        lambda i, found: jnp.where(doc_ref[i] == doc_ref[i + LONG - 1], i, found),
        jnp.int32(0),
    )

    def packed(i):
        return jnp.where(i < LONG, first + i, jnp.where(i - LONG < first, i - LONG, i))

    scale = math.log2(math.e) * HEAD_DIM ** (-0.5)

    def arrange(i):
        at = packed(i)
        here = pl.ds(pl.multiple_of(i * BLOCK, BLOCK), BLOCK)
        there = pl.ds(pl.multiple_of(at * BLOCK, BLOCK), BLOCK)
        key = kv_ref[0, there, :]
        ka[here, 0:128] = key
        ka[here, 128:256] = key
        va[here, 0:128] = kv_ref[1, there, :]
        va[here, 128:256] = jnp.ones((BLOCK, 128), BF16)
        query = q_ref[pl.ds(pl.multiple_of(at * ROWS, ROWS), ROWS), :].astype(F32) * scale
        high = query.astype(BF16)
        rows = pl.ds(pl.multiple_of(i * ROWS, ROWS), ROWS)
        qa[rows, 0:128] = high
        qa[rows, 128:256] = (query - high.astype(F32)).astype(BF16)

    loop(BLOCKS, arrange)

    def attend_rows(rows, base, chunks, docs=None):
        q = qa[rows, :]
        m = total = None
        for c in range(chunks):
            keys = slice(base + c * CHUNK, base + (c + 1) * CHUNK)
            s = lax.dot_general(q, ka[keys, :], (((1,), (1,)), ((), ())), preferred_element_type=F32)
            parts = [s[:, b * 128 : b * 128 + 128] for b in range(CHUNK // 128)]
            if docs is not None:
                for b in range(CHUNK // BLOCK):
                    key_doc = doc_ref[packed(jnp.int32((base + c * CHUNK) // BLOCK + b))]
                    parts[b] = jnp.where(docs == key_doc, parts[b], -1e30)
            top = functools.reduce(jnp.maximum, parts)
            top = jnp.broadcast_to(jnp.max(top, axis=1, keepdims=True), top.shape)
            new_m = top if m is None else jnp.maximum(m, top)
            w = jnp.concatenate([jnp.exp2(part - new_m).astype(BF16) for part in parts], axis=1)
            add = jnp.dot(w, va[keys, :], preferred_element_type=F32)
            if m is None:
                total = add
            else:
                shrink = jnp.exp2(m - new_m)
                total = total * jnp.concatenate([shrink, shrink], axis=1) + add
            m = new_m
        o_ref[rows, :] = (total[:, 0:128] / total[:, 128:256]).astype(BF16)

    def long_tile(t):
        attend_rows(pl.ds(pl.multiple_of(t * TILE, TILE), TILE), 0, LONG_KEYS // CHUNK)

    loop(LONG * ROWS // TILE, long_tile)

    def short_tile(t):
        per = SHORT_TILE // ROWS
        docs = jnp.concatenate(
            [jnp.full((ROWS, 128), doc_ref[packed(LONG + t * per + b)], jnp.int32) for b in range(per)], axis=0
        )
        rows = pl.ds(pl.multiple_of(LONG * ROWS + t * SHORT_TILE, 128), SHORT_TILE)
        attend_rows(rows, LONG_KEYS, SHORT_KEYS // CHUNK, docs)

    loop((BLOCKS - LONG) * ROWS // SHORT_TILE, short_tile)

    lanes = lax.broadcasted_iota(jnp.int32, (PIECE, 128), 1)

    def squares(half):
        part = sq[...]
        high = part.astype(BF16)
        low = (part - high.astype(F32)).astype(BF16)
        ones = jnp.ones((8, 128), BF16)
        dims = (((1,), (1,)), ((), ()))
        sq_ref[:, half * 256 : half * 256 + 256] = lax.dot_general(
            ones, high, dims, preferred_element_type=F32
        ) + lax.dot_general(ones, low, dims, preferred_element_type=F32)
        hot_ref[:, half * 256 : half * 256 + 256] = jnp.transpose(hot[...])[0:DOCS].astype(BF16)

    for half in range(2):
        def move_half(i, half=half):
            p = half * 32 + i
            at = source_ref[p]
            doc = doc_ref[at]
            row = jnp.where(at < first, at + LONG, jnp.where(at < first + LONG, at - first, at))
            piece = o_ref[pl.ds(pl.multiple_of(row * ROWS, ROWS), ROWS), :]
            out_ref[p] = piece
            wide = piece.astype(F32)
            wide = wide * wide
            here = pl.ds(pl.multiple_of(i * PIECE, PIECE), PIECE)
            sq[here, :] = wide[0:8] + wide[8:16] + wide[16:24] + wide[24:32]
            hot[here, :] = (lanes == doc).astype(F32)

        loop(32, move_half)
        squares(half)


def attend(block_doc, block_source, q, kv):
    smem = pl.BlockSpec(memory_space=pltpu.SMEM)
    vmem = pl.BlockSpec(memory_space=pltpu.VMEM)
    return pl.pallas_call(
        attend_kernel,
        out_shape=(
            jax.ShapeDtypeStruct((BLOCKS, ROWS, HEAD_DIM), BF16),
            jax.ShapeDtypeStruct((8, BLOCKS * PIECE), F32),
            jax.ShapeDtypeStruct((DOCS, BLOCKS * PIECE), BF16),
        ),
        in_specs=[smem, smem, vmem, vmem],
        out_specs=(vmem, vmem, vmem),
        scratch_shapes=[
            pltpu.VMEM((BLOCKS * BLOCK, 256), BF16),
            pltpu.VMEM((BLOCKS * BLOCK, 256), BF16),
            pltpu.VMEM((BLOCKS * ROWS, 256), BF16),
            pltpu.VMEM((256, 128), F32),
            pltpu.VMEM((256, 128), F32),
            pltpu.VMEM((BLOCKS * ROWS, HEAD_DIM), BF16),
        ],
        compiler_params=pltpu.CompilerParams(vmem_limit_bytes=48 * 1024 * 1024),
        name="attend",
    )(block_doc, block_source, q, kv)


def collect_kernel(
    o_ref, sq_ref, hot_ref, lat_ref, gain_ref,
    att_ref, emb_ref,
    home, sq_in, doc_out, doc_in, norm_out, norm_in, row_out, row_in,
    s_o, r_o, s_sq, r_sq, s_d, r_d, s_n, r_n, s_e, r_e,
):
    me = Place()
    enter(me, 5)
    me8 = me.plane * 4 + me.kv
    core = me.core
    to_core = me.kv // 2
    half = me.kv % 2

    def partners(src, box, s_sem, r_sem, run):
        def one(i):
            @pl.when(i != me8)
            def _():
                device = me.at(i % 4 + 4 * (me.z // 4), me.y, me.core, i // 4)
                run(send(src, box.at[me8], s_sem.at[i], r_sem.at[me8], device))

        loop(8, one)

    def from_partners(box, r_sem):
        def one(i):
            @pl.when(i != me8)
            def _():
                arrived(box.at[i], r_sem.at[i])

        loop(8, one)

    start = lambda copy: copy.start()
    sent = lambda copy: copy.wait_send()

    partners(sq_ref, sq_in, s_sq, r_sq, start)
    sq_in[me8] = sq_ref[...]

    def result(j, run):
        s = (j + me.ctx) % 32
        src = o_ref.at[pl.ds(2 * s, 2)]
        slot = half * 16 + me.piece
        run(
            me.is_me(s // 4, s % 4, to_core),
            send(src, home.at[slot], s_o.at[s], r_o.at[slot], me.at(s // 4, s % 4, to_core)),
            pltpu.make_async_copy(src, home.at[slot], r_o.at[slot]),
        )

    loop(32, lambda j: result(j, start_either))

    from_partners(sq_in, r_sq)
    channel_total = jnp.sum(sq_in[...], axis=0)[0:1]
    factor = lax.rsqrt(channel_total / CHANNELS + EPS)
    factor = jnp.transpose(jnp.broadcast_to(factor, (128, BLOCKS * PIECE)))
    whole = o_ref[...].astype(F32).reshape(BLOCKS, 4, PIECE, 128)
    normed = []
    for h in range(4):
        part = whole[:, h].reshape(BLOCKS * PIECE, 128)
        normed.append((part * factor * gain_ref[h : h + 1, :]).astype(BF16))
    normed = jnp.concatenate(normed, axis=1)

    lat = lat_ref[...]
    s = lax.dot_general(normed, lat, (((1,), (1,)), ((), ())), preferred_element_type=F32) * 512 ** (-0.5)
    w = jnp.exp(s - jnp.max(s, axis=-1, keepdims=True))
    w = (w / jnp.sum(w, axis=-1, keepdims=True)).astype(BF16)
    by_doc = jnp.dot(hot_ref[...], w, preferred_element_type=F32)
    sums = None
    for _ in range(3):
        part = by_doc.astype(BF16)
        by_doc = by_doc - part.astype(F32)
        add = jnp.dot(part, lat, preferred_element_type=F32)
        sums = add if sums is None else sums + add

    w8 = me.piece % 8
    doc_out[...] = jnp.concatenate(
        [
            sums[two * 8 : two * 8 + 8, h * 128 : h * 128 + 128].reshape(8, 1, 128)
            for two in range(2)
            for h in range(4)
        ],
        axis=1,
    )

    def document(w, run):
        run(
            w == w8,
            send(doc_out.at[w], doc_in.at[w8], s_d.at[w], r_d.at[w8], me.at(me.z, w // 2, w % 2)),
            pltpu.make_async_copy(doc_out.at[w], doc_in.at[w8], r_d.at[w8]),
        )

    loop(8, lambda w: document(w, start_either))
    loop(8, lambda w: arrived(doc_in.at[w], r_d.at[w]))
    row_out[...] = jnp.sum(doc_in[...], axis=0)

    def share(j, run):
        s = (j + me.ctx) % 32
        dst = row_in.at[half, me.piece]
        slot = half * 16 + me.piece
        run(
            me.is_me(s // 4, s % 4, to_core),
            send(row_out, dst, s_e.at[s], r_e.at[slot], me.at(s // 4, s % 4, to_core)),
            pltpu.make_async_copy(row_out, dst, r_e.at[slot]),
        )

    loop(32, lambda j: share(j, start_either))

    loop(32, lambda i: arrived(home.at[i], r_o.at[i]))
    for side in range(2):
        for block in range(2):
            for pair in range(8):
                rows = []
                for part in range(2):
                    piece = home[side * 16 + pair * 2 + part, block].astype(F32)
                    rows.append(jnp.concatenate([piece[h * 8 : h * 8 + 8] for h in range(4)], axis=1))
                at = block * BLOCK + pair * 16
                att_ref[at : at + 16, side * 512 : side * 512 + 512] = jnp.concatenate(rows, axis=0).astype(BF16)

    loop(32, lambda i: arrived(row_in.at[i // 16, i % 16], r_e.at[i]))
    rows = row_in[...]
    rows = rows[:, 0:8] + rows[:, 8:16]
    for two in range(2):
        square = rows[:, :, two * 4 : two * 4 + 4, :]
        square = jnp.sum(square * square, axis=(0, 2))
        norm_out[two] = jnp.broadcast_to(jnp.sum(square, axis=-1, keepdims=True), (8, 128))
    my_head = me.plane * 2 + core

    def head(i, run):
        @pl.when(i != my_head)
        def _():
            device = me.at(me.z, me.y, i % 2, i // 2)
            run(send(norm_out, norm_in.at[my_head], s_n.at[i], r_n.at[my_head], device))

    loop(4, lambda i: head(i, start))
    norm_in[my_head] = norm_out[...]

    def from_head(i):
        @pl.when(i != my_head)
        def _():
            arrived(norm_in.at[i], r_n.at[i])

    loop(4, from_head)
    factors = lax.rsqrt(jnp.sum(norm_in[...], axis=0) / CHANNELS + EPS)
    for side in range(2):
        for h in range(4):
            at = side * 512 + h * 128
            for two in range(2):
                emb_ref[two * 8 : two * 8 + 8, at : at + 128] = rows[side, :, two * 4 + h, :] * factors[two]

    partners(sq_ref, sq_in, s_sq, r_sq, sent)
    loop(4, lambda i: head(i, sent))
    loop(32, lambda j: result(j, end_either))
    loop(8, lambda w: document(w, end_either))
    loop(32, lambda j: share(j, end_either))


def collect(results, squares, hot, latents, gain):
    dma = pltpu.SemaphoreType.DMA
    vmem = pl.BlockSpec(memory_space=pltpu.VMEM)
    return pl.pallas_call(
        collect_kernel,
        out_shape=(
            jax.ShapeDtypeStruct((256, 1024), BF16),
            jax.ShapeDtypeStruct((DOCS, 1024), F32),
        ),
        in_specs=[vmem] * 5,
        out_specs=(vmem, vmem),
        scratch_shapes=[
            pltpu.VMEM((32, 2, ROWS, HEAD_DIM), BF16),
            pltpu.VMEM((8, 8, BLOCKS * PIECE), F32),
            pltpu.VMEM((8, 8, 128), F32),
            pltpu.VMEM((8, 8, 128), F32),
            pltpu.VMEM((2, 8, 128), F32),
            pltpu.VMEM((4, 2, 8, 128), F32),
            pltpu.VMEM((8, 128), F32),
            pltpu.VMEM((2, 16, 8, 128), F32),
            dma((32,)), dma((32,)),
            dma((8,)), dma((8,)),
            dma((8,)), dma((8,)),
            dma((4,)), dma((4,)),
            dma((32,)), dma((32,)),
        ],
        compiler_params=pltpu.CompilerParams(
            collective_id=1, has_side_effects=True, vmem_limit_bytes=40 * 1024 * 1024
        ),
        name="collect",
    )(results, squares, hot, latents, gain)


def shards(queries, keys, values, latents, norm_gain, block_doc, block_source):
    q, kv, lat, gain = spread(queries, keys, values, latents, norm_gain.reshape(2, 4, 128))
    results, squares, hot = attend(block_doc, block_source, q.reshape(BLOCKS * ROWS, HEAD_DIM), kv)
    return collect(results, squares, hot, lat, gain)


def solution(mesh):
    in_specs = (
        P(("dp", "ctx"), "head"),
        P(("dp", "ctx"), "head"),
        P(("dp", "ctx"), "head"),
        P(None, "head"),
        P("head"),
        P("dp"),
        P("dp"),
    )
    out_specs = (P(("dp", "ctx"), "head"), P("dp", "head"))
    return jax.shard_map(shards, mesh=mesh, in_specs=in_specs, out_specs=out_specs, check_vma=False)
```

```python
import functools
import math

import jax
import jax.numpy as jnp
from jax import lax
from jax.experimental import pallas as pl
from jax.experimental.pallas import tpu as pltpu
from jax.sharding import PartitionSpec as P

HEADS = 32
HEAD_DIM = 128
BLOCK = 128
BLOCKS = 64
LONG = 40
DOCS = 16
CHANNELS = HEADS * HEAD_DIM
PIECE = 8
ROWS = 4 * PIECE
TILE = 640
SHORT_TILE = 384
CHUNK = 256
LONG_KEYS = LONG * BLOCK
SHORT_KEYS = (BLOCKS - LONG) * BLOCK
EPS = 1e-05
PARTS = 1
PART = 256 // PARTS
HALF = PART // 2
AHEAD = 4
Q_START = 4
Q_STEP = 4
LAG = 4
MESH = pl.DeviceIdType.MESH
F32 = jnp.float32
BF16 = jnp.bfloat16


def loop(count, body):
    def step(i, carry):
        body(i)
        return carry

    lax.fori_loop(0, count, step, 0)


class Place:
    def __init__(self):
        self.ctx = lax.axis_index("ctx")
        head = lax.axis_index("head")
        self.z = self.ctx // 4
        self.y = self.ctx % 4
        self.plane = head // 2
        self.core = head % 2
        self.kv = self.z % 4
        self.piece = (self.z // 4) * 8 + self.y * 2 + self.core

    def at(self, z, y, core, plane=None):
        plane = self.plane if plane is None else plane
        return {"ctx": z * 4 + y, "head": plane * 2 + core}

    def worker(self, kv, piece):
        return (kv + 4 * (piece // 8), (piece % 8) // 2, piece % 2)

    def is_me(self, z, y, core):
        return (z == self.z) & (y == self.y) & (core == self.core)


def greet(me):
    barrier = pltpu.get_barrier_semaphore()

    def one(i):
        z, y, core = i // 8, (i // 2) % 4, i % 2

        @pl.when(jnp.logical_not(me.is_me(z, y, core)))
        def _():
            pl.semaphore_signal(barrier, 1, device_id=me.at(z, y, core), device_id_type=MESH)

    def other(i):
        here = i == 4
        z = jnp.where(here, me.z, i % 4 + 4 * (me.z // 4))
        core = jnp.where(here, 1 - me.core, me.core)
        pl.semaphore_signal(barrier, 1, device_id=me.at(z, me.y, core, 1 - me.plane), device_id_type=MESH)

    loop(64, one)
    loop(5, other)
    return barrier


def send(src, dst, send_sem, recv_sem, device):
    return pltpu.make_async_remote_copy(
        src_ref=src, dst_ref=dst, send_sem=send_sem, recv_sem=recv_sem, device_id=device, device_id_type=MESH
    )


def arrived(ref, sem):
    pltpu.make_async_copy(ref, ref, sem).wait()


def start_either(here, remote, local):
    @pl.when(here)
    def _():
        local.start()

    @pl.when(jnp.logical_not(here))
    def _():
        remote.start()


def end_either(here, remote, local):
    @pl.when(jnp.logical_not(here))
    def _():
        remote.wait_send()


def kernel(
    doc_ref, source_ref, q_ref, k_ref, v_ref, lat_ref, gain_ref,
    att_ref, emb_ref,
    q_in, qs, qp, kv, lat_in, gain_in, ka, va, qa, o_ref, res,
    home, sq_out, sq_in, doc_out, doc_in, norm_out, norm_in, row_out, row_in,
    s_a, r_a, s_b, r_b, s_c, r_c, s_s, r_s, s_q, r_q, s_l, r_l, l_q,
    s_o, r_o, s_sq, r_sq, s_d, r_d, s_n, r_n, s_e, r_e,
):
    me = Place()
    z, y, core = me.z, me.y, me.core
    load_q = pltpu.make_async_copy(q_ref, q_in, l_q)
    load_q.start()
    barrier = greet(me)

    load_q.wait()

    def regroup(i):
        half, pair = i // 8, i % 8
        rows_at = pl.ds(pl.multiple_of(pair * 16, 16), 16)
        for block in range(2):
            tile = q_in[block, rows_at, pl.ds(pl.multiple_of(half * 512, 512), 512)].astype(F32)
            for part in range(2):
                rows = tile[part * 8 : part * 8 + 8]
                rows = jnp.concatenate([rows[:, h * 128 : h * 128 + 128] for h in range(4)], axis=0)
                qs[2 * i + part, block * ROWS : block * ROWS + ROWS, :] = rows.astype(BF16)

    loop(16, regroup)
    va[:, :, 128:256] = jnp.ones((BLOCKS, BLOCK, 128), BF16)

    first = jnp.int32(0)
    for i in range(BLOCKS - LONG + 1):
        first = jnp.where(doc_ref[i] == doc_ref[i + LONG - 1], i, first)

    def packed(i):
        return jnp.where(i < LONG, first + i, jnp.where(i - LONG < first, i - LONG, i))

    def sorted_place(at):
        return jnp.where(at < first, at + LONG, jnp.where(at < first + LONG, at - first, at))

    pl.semaphore_wait(barrier, 68)

    up, down = (y + 1) % 4, (y + 3) % 4
    mine = me.kv // 2 == core

    def order(j):
        odd = j % 2
        return odd * ((j + 1) // 2) + (1 - odd) * (8 - j // 2)

    def column(j, run):
        to_z = (z + order(j)) % 8

        @pl.when((to_z % 4) // 2 == core)
        def _():
            half = to_z % 2
            for part in range(PARTS):
                for kind in range(2):
                    first = part * PART
                    columns = pl.ds(pl.multiple_of(half * HEAD_DIM, HEAD_DIM), HEAD_DIM)
                    src = (k_ref, v_ref)[kind].at[pl.ds(first, PART), columns]
                    dst = kv.at[kind, pl.ds(pl.multiple_of(me.ctx * 256 + first, PART), PART), :]
                    sem = r_a.at[part, z]
                    here = (to_z == z) & (core == kind)
                    copy = send(src, dst, s_a.at[part, kind, to_z], sem, me.at(to_z, y, kind))
                    run(here, copy, pltpu.make_async_copy(src, dst, sem))

    loop(AHEAD, lambda j: column(j, start_either))

    def query(j, run):
        i = (j + me.ctx) % 32
        to = me.worker(2 * core + i // 16, i % 16)
        run(
            me.is_me(*to),
            send(qs.at[i], qp.at[me.ctx], s_q.at[i], r_q.at[me.ctx], me.at(*to)),
            pltpu.make_async_copy(qs.at[i], qp.at[me.ctx], r_q.at[me.ctx]),
        )

    def rows_of(from_z, from_y, first=0, count=256):
        start = pl.multiple_of((from_z * 4 + from_y) * 256 + first, HALF)
        return kv.at[core, pl.ds(start, count), :]

    def to_core(from_z):
        rows = kv.at[core, pl.ds(pl.multiple_of(from_z * 1024, 1024), 1024), :]
        return send(rows, rows, s_s.at[from_z], r_s.at[from_z], me.at(z, y, 1 - core))

    def near(from_z, part):
        rows = rows_of(from_z, y, part * PART, PART)
        return (
            send(rows, rows, s_b.at[0, part, from_z], r_b.at[0, part, from_z], me.at(z, up, core)),
            send(rows, rows, s_b.at[1, part, from_z], r_b.at[1, part, from_z], me.at(z, down, core)),
        )

    def onward(from_z, part):
        one = rows_of(from_z, down, part * PART, HALF)
        two = rows_of(from_z, up, part * PART + HALF, HALF)
        return (
            send(one, one, s_c.at[0, part, from_z], r_c.at[0, part, from_z], me.at(z, up, core)),
            send(two, two, s_c.at[1, part, from_z], r_c.at[1, part, from_z], me.at(z, down, core)),
        )

    steps = 8 * PARTS

    def at_step(e):
        return (z + order(e // PARTS)) % 8, e % PARTS

    def ring(e):
        @pl.when(e < steps)
        def _():
            @pl.when((e % PARTS == 0) & (e // PARTS + AHEAD < 8))
            def _():
                column(e // PARTS + AHEAD, start_either)

            from_z, part = at_step(e)
            arrived(rows_of(from_z, y, part * PART, PART), r_a.at[part, from_z])
            for copy in near(from_z, part):
                copy.start()

        @pl.when((e >= Q_START) & (e < Q_START + 32 // Q_STEP))
        def _():
            for i in range(Q_STEP):
                query((e - Q_START) * Q_STEP + i, start_either)

        @pl.when((e >= LAG) & (e < steps + LAG))
        def _():
            from_z, part = at_step(e - LAG)
            copies = onward(from_z, part)
            arrived(rows_of(from_z, down, part * PART, PART), r_b.at[0, part, from_z])
            copies[0].start()
            arrived(rows_of(from_z, up, part * PART, PART), r_b.at[1, part, from_z])
            copies[1].start()

        @pl.when(e >= 2 * LAG)
        def _():
            from_z, part = at_step(e - 2 * LAG)
            opposite = (y + 2) % 4
            arrived(rows_of(from_z, opposite, part * PART, HALF), r_c.at[0, part, from_z])
            arrived(rows_of(from_z, opposite, part * PART + HALF, HALF), r_c.at[1, part, from_z])

            @pl.when(part == PARTS - 1)
            def _():
                to_core(from_z).start()

    loop(steps + 2 * LAG, ring)

    def pool_inputs():
        other = me.at(z, y, 1 - core)
        half = me.kv % 2
        lat = lat_ref.at[:, pl.ds(pl.multiple_of(half * 512, 512), 512)]
        gain = gain_ref.at[half]
        return (
            pltpu.make_async_copy(lat, lat_in, r_l.at[0]),
            pltpu.make_async_copy(gain, gain_in, r_l.at[1]),
            send(lat, lat_in, s_l.at[0], r_l.at[0], other),
            send(gain, gain_in, s_l.at[1], r_l.at[1], other),
        )

    @pl.when(mine)
    def _():
        for copy in pool_inputs():
            copy.start()

    def sends_done():
        loop(8, lambda j: column(j, end_either))

        def ring_done(e):
            from_z, part = at_step(e)
            for copy in near(from_z, part) + onward(from_z, part):
                copy.wait_send()

        loop(steps, ring_done)
        loop(32, lambda j: query(j, end_either))
        loop(8, lambda from_z: to_core(from_z).wait_send())

        @pl.when(mine)
        def _():
            for copy in pool_inputs()[2:]:
                copy.wait_send()

    def arrange_keys(j):
        from_z = (z + order(j)) % 8
        rows = pl.ds(pl.multiple_of(from_z * 1024, 1024), 1024)
        blocks = pl.ds(from_z * 8, 8)
        arrived(kv.at[1 - core, rows, :], r_s.at[from_z])
        key = kv[0, rows, :].reshape(8, BLOCK, 128)
        ka[blocks, :, 0:128] = key
        ka[blocks, :, 128:256] = key
        va[blocks, :, 0:128] = kv[1, rows, :].reshape(8, BLOCK, 128)

    scale = math.log2(math.e) * HEAD_DIM ** (-0.5)

    def arrange_queries(s):
        arrived(qp.at[s], r_q.at[s])
        query = qp[s].reshape(2, ROWS, 128).astype(F32) * scale
        high = query.astype(BF16)
        blocks = pl.ds(2 * s, 2)
        qa[blocks, :, 0:128] = high
        qa[blocks, :, 128:256] = (query - high.astype(F32)).astype(BF16)

    loop(32, arrange_queries)
    loop(8, arrange_keys)

    sends_done()
    for copy in pool_inputs()[:2]:
        copy.wait()

    def blocks_of(ref, first_block, count):
        return jnp.concatenate([ref[packed(first_block + b)] for b in range(count)], axis=0)

    def attend_rows(q, keys_at, chunks, rows, docs=None):
        m = total = None
        for c in range(chunks):
            key, value, key_docs = keys_at(c)
            s = lax.dot_general(q, key, (((1,), (1,)), ((), ())), preferred_element_type=F32)
            parts = [s[:, b * 128 : b * 128 + 128] for b in range(CHUNK // 128)]
            if docs is not None:
                parts = [jnp.where(docs == doc, part, -1e30) for doc, part in zip(key_docs, parts)]
            top = functools.reduce(jnp.maximum, parts)
            top = jnp.broadcast_to(jnp.max(top, axis=1, keepdims=True), top.shape)
            new_m = top if m is None else jnp.maximum(m, top)
            w = jnp.concatenate([jnp.exp2(part - new_m).astype(BF16) for part in parts], axis=1)
            add = jnp.dot(w, value, preferred_element_type=F32)
            if m is None:
                total = add
            else:
                shrink = jnp.exp2(m - new_m)
                total = total * jnp.concatenate([shrink, shrink], axis=1) + add
            m = new_m
        o_ref[rows] = (total[:, 0:128] / total[:, 128:256]).astype(BF16).reshape(-1, ROWS, 128)

    per_chunk = CHUNK // BLOCK

    def long_keys(c):
        return blocks_of(ka, c * per_chunk, per_chunk), blocks_of(va, c * per_chunk, per_chunk), None

    def long_tile(t):
        per = TILE // ROWS
        attend_rows(blocks_of(qa, t * per, per), long_keys, LONG_KEYS // CHUNK, pl.ds(t * per, per))

    def short_keys(c):
        at = LONG + c * per_chunk
        docs = [doc_ref[packed(at + b)] for b in range(per_chunk)]
        return blocks_of(ka, at, per_chunk), blocks_of(va, at, per_chunk), docs

    def short_tile(t):
        per = SHORT_TILE // ROWS
        at = LONG + t * per
        docs = jnp.concatenate([jnp.full((ROWS, 128), doc_ref[packed(at + b)], jnp.int32) for b in range(per)], axis=0)
        attend_rows(blocks_of(qa, at, per), short_keys, SHORT_KEYS // CHUNK, pl.ds(at, per), docs)

    loop((BLOCKS - LONG) * ROWS // SHORT_TILE, short_tile)
    loop(LONG * ROWS // TILE, long_tile)

    whole = o_ref[...].astype(F32).reshape(BLOCKS, 4, PIECE, 128)
    square = jnp.sum(whole * whole, axis=1).reshape(BLOCKS * PIECE, 128)
    high = square.astype(BF16)
    low = (square - high.astype(F32)).astype(BF16)
    ones = jnp.ones((8, 128), BF16)
    dims = (((1,), (1,)), ((), ()))
    sq_out[...] = lax.dot_general(ones, high, dims, preferred_element_type=F32) + lax.dot_general(
        ones, low, dims, preferred_element_type=F32
    )

    me8 = me.plane * 4 + me.kv
    home_core = me.kv // 2
    half = me.kv % 2

    def partners(src, box, s_sem, r_sem, run):
        def one(i):
            @pl.when(i != me8)
            def _():
                device = me.at(i % 4 + 4 * (me.z // 4), me.y, me.core, i // 4)
                run(send(src, box.at[me8], s_sem.at[i], r_sem.at[me8], device))

        loop(8, one)

    def from_partners(box, r_sem):
        def one(i):
            @pl.when(i != me8)
            def _():
                arrived(box.at[i], r_sem.at[i])

        loop(8, one)

    start = lambda copy: copy.start()
    sent = lambda copy: copy.wait_send()

    partners(sq_out, sq_in, s_sq, r_sq, start)
    sq_in[me8] = sq_out[...]

    def result(j, run):
        s = (j + me.ctx) % 32
        src = res.at[pl.ds(2 * s, 2)]
        slot = half * 16 + me.piece
        run(
            me.is_me(s // 4, s % 4, home_core),
            send(src, home.at[slot], s_o.at[s], r_o.at[slot], me.at(s // 4, s % 4, home_core)),
            pltpu.make_async_copy(src, home.at[slot], r_o.at[slot]),
        )

    def move(p):
        res[p] = o_ref[sorted_place(source_ref[p])]

    loop(BLOCKS, move)
    loop(32, lambda j: result(j, start_either))

    from_partners(sq_in, r_sq)
    channel_total = jnp.sum(sq_in[...], axis=0)[0:1]
    factor = lax.rsqrt(channel_total / CHANNELS + EPS)
    factor = jnp.transpose(jnp.broadcast_to(factor, (128, BLOCKS * PIECE)))
    whole = o_ref[...].astype(F32).reshape(BLOCKS, 4, PIECE, 128)
    normed = []
    for h in range(4):
        part = whole[:, h].reshape(BLOCKS * PIECE, 128)
        normed.append((part * factor * gain_in[h : h + 1, :]).astype(BF16))
    normed = jnp.concatenate(normed, axis=1)

    lat = lat_in[...]
    s = lax.dot_general(normed, lat, (((1,), (1,)), ((), ())), preferred_element_type=F32) * 512 ** (-0.5)
    w = jnp.exp(s - jnp.max(s, axis=-1, keepdims=True))
    w = (w / jnp.sum(w, axis=-1, keepdims=True)).astype(BF16)
    tokens = lax.broadcasted_iota(jnp.int32, (DOCS, PIECE), 0)
    hot = jnp.concatenate(
        [(tokens == doc_ref[packed(i)]).astype(F32) for i in range(BLOCKS)], axis=1
    ).astype(BF16)
    by_doc = jnp.dot(hot, w, preferred_element_type=F32)
    sums = None
    for _ in range(3):
        part = by_doc.astype(BF16)
        by_doc = by_doc - part.astype(F32)
        add = jnp.dot(part, lat, preferred_element_type=F32)
        sums = add if sums is None else sums + add

    w8 = me.piece % 8
    doc_out[...] = jnp.concatenate(
        [
            sums[two * 8 : two * 8 + 8, h * 128 : h * 128 + 128].reshape(8, 1, 128)
            for two in range(2)
            for h in range(4)
        ],
        axis=1,
    )

    def document(w, run):
        run(
            w == w8,
            send(doc_out.at[w], doc_in.at[w8], s_d.at[w], r_d.at[w8], me.at(me.z, w // 2, w % 2)),
            pltpu.make_async_copy(doc_out.at[w], doc_in.at[w8], r_d.at[w8]),
        )

    loop(8, lambda w: document(w, start_either))
    loop(8, lambda w: arrived(doc_in.at[w], r_d.at[w]))
    row_out[...] = jnp.sum(doc_in[...], axis=0)

    def share(j, run):
        s = (j + me.ctx) % 32
        dst = row_in.at[half, me.piece]
        slot = half * 16 + me.piece
        run(
            me.is_me(s // 4, s % 4, home_core),
            send(row_out, dst, s_e.at[s], r_e.at[slot], me.at(s // 4, s % 4, home_core)),
            pltpu.make_async_copy(row_out, dst, r_e.at[slot]),
        )

    loop(32, lambda j: share(j, start_either))

    loop(32, lambda i: arrived(home.at[i], r_o.at[i]))
    for side in range(2):
        for block in range(2):
            for pair in range(8):
                rows = []
                for part in range(2):
                    piece = home[side * 16 + pair * 2 + part, block].astype(F32)
                    rows.append(jnp.concatenate([piece[h * 8 : h * 8 + 8] for h in range(4)], axis=1))
                at = block * BLOCK + pair * 16
                att_ref[at : at + 16, side * 512 : side * 512 + 512] = jnp.concatenate(rows, axis=0).astype(BF16)

    loop(32, lambda i: arrived(row_in.at[i // 16, i % 16], r_e.at[i]))
    rows = row_in[...]
    rows = rows[:, 0:8] + rows[:, 8:16]
    for two in range(2):
        square = rows[:, :, two * 4 : two * 4 + 4, :]
        square = jnp.sum(square * square, axis=(0, 2))
        norm_out[two] = jnp.broadcast_to(jnp.sum(square, axis=-1, keepdims=True), (8, 128))
    my_head = me.plane * 2 + core

    def head(i, run):
        @pl.when(i != my_head)
        def _():
            device = me.at(me.z, me.y, i % 2, i // 2)
            run(send(norm_out, norm_in.at[my_head], s_n.at[i], r_n.at[my_head], device))

    loop(4, lambda i: head(i, start))
    norm_in[my_head] = norm_out[...]

    def from_head(i):
        @pl.when(i != my_head)
        def _():
            arrived(norm_in.at[i], r_n.at[i])

    loop(4, from_head)
    factors = lax.rsqrt(jnp.sum(norm_in[...], axis=0) / CHANNELS + EPS)
    for side in range(2):
        for h in range(4):
            at = side * 512 + h * 128
            for two in range(2):
                emb_ref[two * 8 : two * 8 + 8, at : at + 128] = rows[side, :, two * 4 + h, :] * factors[two]

    partners(sq_out, sq_in, s_sq, r_sq, sent)
    loop(4, lambda i: head(i, sent))
    loop(32, lambda j: result(j, end_either))
    loop(8, lambda w: document(w, end_either))
    loop(32, lambda j: share(j, end_either))


def shards(queries, keys, values, latents, norm_gain, block_doc, block_source):
    dma = pltpu.SemaphoreType.DMA
    hbm = pl.BlockSpec(memory_space=pltpu.HBM)
    vmem = pl.BlockSpec(memory_space=pltpu.VMEM)
    smem = pl.BlockSpec(memory_space=pltpu.SMEM)
    tokens = BLOCKS * BLOCK
    return pl.pallas_call(
        kernel,
        out_shape=(
            jax.ShapeDtypeStruct((256, 1024), BF16),
            jax.ShapeDtypeStruct((DOCS, 1024), F32),
        ),
        in_specs=[smem, smem] + [hbm] * 5,
        out_specs=(vmem, vmem),
        scratch_shapes=[
            pltpu.VMEM((2, BLOCK, 1024), BF16),
            pltpu.VMEM((32, 2 * ROWS, HEAD_DIM), BF16),
            pltpu.VMEM((32, 2 * ROWS, HEAD_DIM), BF16),
            pltpu.VMEM((2, tokens, HEAD_DIM), BF16),
            pltpu.VMEM((512, 512), BF16),
            pltpu.VMEM((4, 128), F32),
            pltpu.VMEM((BLOCKS, BLOCK, 256), BF16),
            pltpu.VMEM((BLOCKS, BLOCK, 256), BF16),
            pltpu.VMEM((BLOCKS, ROWS, 256), BF16),
            pltpu.VMEM((BLOCKS, ROWS, HEAD_DIM), BF16),
            pltpu.VMEM((BLOCKS, ROWS, HEAD_DIM), BF16),
            pltpu.VMEM((32, 2, ROWS, HEAD_DIM), BF16),
            pltpu.VMEM((8, BLOCKS * PIECE), F32),
            pltpu.VMEM((8, 8, BLOCKS * PIECE), F32),
            pltpu.VMEM((8, 8, 128), F32),
            pltpu.VMEM((8, 8, 128), F32),
            pltpu.VMEM((2, 8, 128), F32),
            pltpu.VMEM((4, 2, 8, 128), F32),
            pltpu.VMEM((8, 128), F32),
            pltpu.VMEM((2, 16, 8, 128), F32),
            dma((PARTS, 2, 8)), dma((PARTS, 8)),
            dma((2, PARTS, 8)), dma((2, PARTS, 8)),
            dma((2, PARTS, 8)), dma((2, PARTS, 8)),
            dma((8,)), dma((8,)),
            dma((32,)), dma((32,)),
            dma((2,)), dma((2,)),
            dma,
            dma((32,)), dma((32,)),
            dma((8,)), dma((8,)),
            dma((8,)), dma((8,)),
            dma((4,)), dma((4,)),
            dma((32,)), dma((32,)),
        ],
        compiler_params=pltpu.CompilerParams(
            collective_id=0, has_side_effects=True, vmem_limit_bytes=60 * 1024 * 1024
        ),
        name="embed",
    )(
        block_doc, block_source, queries.reshape(2, BLOCK, 1024), keys, values, latents, norm_gain.reshape(2, 4, 128)
    )


def solution(mesh):
    in_specs = (
        P(("dp", "ctx"), "head"),
        P(("dp", "ctx"), "head"),
        P(("dp", "ctx"), "head"),
        P(None, "head"),
        P("head"),
        P("dp"),
        P("dp"),
    )
    out_specs = (P(("dp", "ctx"), "head"), P("dp", "head"))
    return jax.shard_map(shards, mesh=mesh, in_specs=in_specs, out_specs=out_specs, check_vma=False)
```

```python
import functools
import math

import jax
import jax.numpy as jnp
from jax import lax
from jax.experimental import pallas as pl
from jax.experimental.pallas import tpu as pltpu
from jax.sharding import PartitionSpec as P

HEADS = 32
HEAD_DIM = 128
BLOCK = 128
BLOCKS = 64
LONG = 40
DOCS = 16
CHANNELS = HEADS * HEAD_DIM
PIECE = 8
ROWS = 4 * PIECE
TILE = 640
SHORT_TILE = 384
CHUNK = 256
LONG_KEYS = LONG * BLOCK
SHORT_KEYS = (BLOCKS - LONG) * BLOCK
EPS = 1e-05
OUT_1, OUT_2 = 14, 8
PARTS = 1
PART = 256 // PARTS
HALF = PART // 2
AHEAD = 4
Q_START = 4
Q_STEP = 4
LAG = 4
MESH = pl.DeviceIdType.MESH
F32 = jnp.float32
BF16 = jnp.bfloat16


def loop(count, body):
    def step(i, carry):
        body(i)
        return carry

    lax.fori_loop(0, count, step, 0)


class Place:
    def __init__(self):
        self.ctx = lax.axis_index("ctx")
        head = lax.axis_index("head")
        self.z = self.ctx // 4
        self.y = self.ctx % 4
        self.plane = head // 2
        self.core = head % 2
        self.kv = self.z % 4
        self.piece = (self.z // 4) * 8 + self.y * 2 + self.core

    def at(self, z, y, core, plane=None):
        plane = self.plane if plane is None else plane
        return {"ctx": z * 4 + y, "head": plane * 2 + core}

    def worker(self, kv, piece):
        return (kv + 4 * (piece // 8), (piece % 8) // 2, piece % 2)

    def is_me(self, z, y, core):
        return (z == self.z) & (y == self.y) & (core == self.core)


def greet(me):
    barrier = pltpu.get_barrier_semaphore()

    def one(i):
        z, y, core = i // 8, (i // 2) % 4, i % 2

        @pl.when(jnp.logical_not(me.is_me(z, y, core)))
        def _():
            pl.semaphore_signal(barrier, 1, device_id=me.at(z, y, core), device_id_type=MESH)

    def other(i):
        here = i == 4
        z = jnp.where(here, me.z, i % 4 + 4 * (me.z // 4))
        core = jnp.where(here, 1 - me.core, me.core)
        pl.semaphore_signal(barrier, 1, device_id=me.at(z, me.y, core, 1 - me.plane), device_id_type=MESH)

    loop(64, one)
    loop(5, other)
    return barrier


def send(src, dst, send_sem, recv_sem, device):
    return pltpu.make_async_remote_copy(
        src_ref=src, dst_ref=dst, send_sem=send_sem, recv_sem=recv_sem, device_id=device, device_id_type=MESH
    )


def arrived(ref, sem):
    pltpu.make_async_copy(ref, ref, sem).wait()


def start_either(here, remote, local):
    @pl.when(here)
    def _():
        local.start()

    @pl.when(jnp.logical_not(here))
    def _():
        remote.start()


def end_either(here, remote, local):
    @pl.when(jnp.logical_not(here))
    def _():
        remote.wait_send()


def kernel(
    doc_ref, source_ref, q_ref, k_ref, v_ref, lat_ref, gain_ref,
    att_ref, emb_ref,
    q_in, qs, qp, kv, lat_in, gain_in, ka, va, qa, o_ref, res,
    home, sq_out, sq_in, doc_out, doc_in, norm_out, norm_in, row_out, row_in,
    s_a, r_a, s_b, r_b, s_c, r_c, s_s, r_s, s_q, r_q, s_l, r_l, l_q,
    s_o, r_o, s_sq, r_sq, s_d, r_d, s_n, r_n, s_e, r_e,
):
    me = Place()
    z, y, core = me.z, me.y, me.core
    load_q = pltpu.make_async_copy(q_ref, q_in, l_q)
    load_q.start()
    barrier = greet(me)

    load_q.wait()

    def regroup(i):
        half, pair = i // 8, i % 8
        rows_at = pl.ds(pl.multiple_of(pair * 16, 16), 16)
        for block in range(2):
            tile = q_in[block, rows_at, pl.ds(pl.multiple_of(half * 512, 512), 512)].astype(F32)
            for part in range(2):
                rows = tile[part * 8 : part * 8 + 8]
                rows = jnp.concatenate([rows[:, h * 128 : h * 128 + 128] for h in range(4)], axis=0)
                qs[2 * i + part, block * ROWS : block * ROWS + ROWS, :] = rows.astype(BF16)

    loop(16, regroup)
    va[:, :, 128:256] = jnp.ones((BLOCKS, BLOCK, 128), BF16)

    first = jnp.int32(0)
    for i in range(BLOCKS - LONG + 1):
        first = jnp.where(doc_ref[i] == doc_ref[i + LONG - 1], i, first)

    def packed(i):
        return jnp.where(i < LONG, first + i, jnp.where(i - LONG < first, i - LONG, i))

    def sorted_place(at):
        return jnp.where(at < first, at + LONG, jnp.where(at < first + LONG, at - first, at))

    pl.semaphore_wait(barrier, 68)

    up, down = (y + 1) % 4, (y + 3) % 4
    mine = me.kv // 2 == core

    def order(j):
        odd = j % 2
        return odd * ((j + 1) // 2) + (1 - odd) * (8 - j // 2)

    def column(j, run):
        to_z = (z + order(j)) % 8

        @pl.when((to_z % 4) // 2 == core)
        def _():
            half = to_z % 2
            for part in range(PARTS):
                for kind in range(2):
                    first = part * PART
                    columns = pl.ds(pl.multiple_of(half * HEAD_DIM, HEAD_DIM), HEAD_DIM)
                    src = (k_ref, v_ref)[kind].at[pl.ds(first, PART), columns]
                    dst = kv.at[kind, pl.ds(pl.multiple_of(me.ctx * 256 + first, PART), PART), :]
                    sem = r_a.at[part, z]
                    here = (to_z == z) & (core == kind)
                    copy = send(src, dst, s_a.at[part, kind, to_z], sem, me.at(to_z, y, kind))
                    run(here, copy, pltpu.make_async_copy(src, dst, sem))

    loop(AHEAD, lambda j: column(j, start_either))

    def query(j, run):
        i = (j + me.ctx) % 32
        to = me.worker(2 * core + i // 16, i % 16)
        run(
            me.is_me(*to),
            send(qs.at[i], qp.at[me.ctx], s_q.at[i], r_q.at[me.ctx], me.at(*to)),
            pltpu.make_async_copy(qs.at[i], qp.at[me.ctx], r_q.at[me.ctx]),
        )

    def rows_of(from_z, from_y, first=0, count=256):
        start = pl.multiple_of((from_z * 4 + from_y) * 256 + first, HALF)
        return kv.at[core, pl.ds(start, count), :]

    def to_core(from_z):
        rows = kv.at[core, pl.ds(pl.multiple_of(from_z * 1024, 1024), 1024), :]
        return send(rows, rows, s_s.at[from_z], r_s.at[from_z], me.at(z, y, 1 - core))

    def near(from_z, part):
        rows = rows_of(from_z, y, part * PART, PART)
        return (
            send(rows, rows, s_b.at[0, part, from_z], r_b.at[0, part, from_z], me.at(z, up, core)),
            send(rows, rows, s_b.at[1, part, from_z], r_b.at[1, part, from_z], me.at(z, down, core)),
        )

    def onward(from_z, part):
        one = rows_of(from_z, down, part * PART, HALF)
        two = rows_of(from_z, up, part * PART + HALF, HALF)
        return (
            send(one, one, s_c.at[0, part, from_z], r_c.at[0, part, from_z], me.at(z, up, core)),
            send(two, two, s_c.at[1, part, from_z], r_c.at[1, part, from_z], me.at(z, down, core)),
        )

    steps = 8 * PARTS

    def at_step(e):
        return (z + order(e // PARTS)) % 8, e % PARTS

    def ring(e):
        @pl.when(e < steps)
        def _():
            @pl.when((e % PARTS == 0) & (e // PARTS + AHEAD < 8))
            def _():
                column(e // PARTS + AHEAD, start_either)

            from_z, part = at_step(e)
            arrived(rows_of(from_z, y, part * PART, PART), r_a.at[part, from_z])
            for copy in near(from_z, part):
                copy.start()

        @pl.when((e >= Q_START) & (e < Q_START + 32 // Q_STEP))
        def _():
            for i in range(Q_STEP):
                query((e - Q_START) * Q_STEP + i, start_either)

        @pl.when((e >= LAG) & (e < steps + LAG))
        def _():
            from_z, part = at_step(e - LAG)
            copies = onward(from_z, part)
            arrived(rows_of(from_z, down, part * PART, PART), r_b.at[0, part, from_z])
            copies[0].start()
            arrived(rows_of(from_z, up, part * PART, PART), r_b.at[1, part, from_z])
            copies[1].start()

        @pl.when(e >= 2 * LAG)
        def _():
            from_z, part = at_step(e - 2 * LAG)
            opposite = (y + 2) % 4
            arrived(rows_of(from_z, opposite, part * PART, HALF), r_c.at[0, part, from_z])
            arrived(rows_of(from_z, opposite, part * PART + HALF, HALF), r_c.at[1, part, from_z])

            @pl.when(part == PARTS - 1)
            def _():
                to_core(from_z).start()

    loop(steps + 2 * LAG, ring)

    def pool_inputs():
        other = me.at(z, y, 1 - core)
        half = me.kv % 2
        lat = lat_ref.at[:, pl.ds(pl.multiple_of(half * 512, 512), 512)]
        gain = gain_ref.at[half]
        return (
            pltpu.make_async_copy(lat, lat_in, r_l.at[0]),
            pltpu.make_async_copy(gain, gain_in, r_l.at[1]),
            send(lat, lat_in, s_l.at[0], r_l.at[0], other),
            send(gain, gain_in, s_l.at[1], r_l.at[1], other),
        )

    @pl.when(mine)
    def _():
        for copy in pool_inputs():
            copy.start()

    def sends_done():
        loop(8, lambda j: column(j, end_either))

        def ring_done(e):
            from_z, part = at_step(e)
            for copy in near(from_z, part) + onward(from_z, part):
                copy.wait_send()

        loop(steps, ring_done)
        loop(32, lambda j: query(j, end_either))
        loop(8, lambda from_z: to_core(from_z).wait_send())

        @pl.when(mine)
        def _():
            for copy in pool_inputs()[2:]:
                copy.wait_send()

    def arrange_keys(j):
        from_z = (z + order(j)) % 8
        rows = pl.ds(pl.multiple_of(from_z * 1024, 1024), 1024)
        blocks = pl.ds(from_z * 8, 8)
        arrived(kv.at[1 - core, rows, :], r_s.at[from_z])
        key = kv[0, rows, :].reshape(8, BLOCK, 128)
        ka[blocks, :, 0:128] = key
        ka[blocks, :, 128:256] = key
        va[blocks, :, 0:128] = kv[1, rows, :].reshape(8, BLOCK, 128)

    scale = math.log2(math.e) * HEAD_DIM ** (-0.5)

    def arrange_queries(s):
        arrived(qp.at[s], r_q.at[s])
        query = qp[s].reshape(2, ROWS, 128).astype(F32) * scale
        high = query.astype(BF16)
        blocks = pl.ds(2 * s, 2)
        qa[blocks, :, 0:128] = high
        qa[blocks, :, 128:256] = (query - high.astype(F32)).astype(BF16)

    loop(32, arrange_queries)
    loop(8, arrange_keys)

    for copy in pool_inputs()[:2]:
        copy.wait()

    def blocks_of(ref, first_block, count):
        return jnp.concatenate([ref[packed(first_block + b)] for b in range(count)], axis=0)

    def attend_rows(q, keys_at, chunks, rows, docs=None):
        m = total = None
        for c in range(chunks):
            key, value, key_docs = keys_at(c)
            s = lax.dot_general(q, key, (((1,), (1,)), ((), ())), preferred_element_type=F32)
            parts = [s[:, b * 128 : b * 128 + 128] for b in range(CHUNK // 128)]
            if docs is not None:
                parts = [jnp.where(docs == doc, part, -1e30) for doc, part in zip(key_docs, parts)]
            top = functools.reduce(jnp.maximum, parts)
            top = jnp.broadcast_to(jnp.max(top, axis=1, keepdims=True), top.shape)
            new_m = top if m is None else jnp.maximum(m, top)
            w = jnp.concatenate([jnp.exp2(part - new_m).astype(BF16) for part in parts], axis=1)
            add = jnp.dot(w, value, preferred_element_type=F32)
            if m is None:
                total = add
            else:
                shrink = jnp.exp2(m - new_m)
                total = total * jnp.concatenate([shrink, shrink], axis=1) + add
            m = new_m
        o_ref[rows] = (total[:, 0:128] / total[:, 128:256]).astype(BF16).reshape(-1, ROWS, 128)

    per_chunk = CHUNK // BLOCK

    def long_keys(c):
        return blocks_of(ka, c * per_chunk, per_chunk), blocks_of(va, c * per_chunk, per_chunk), None

    def long_tile(t):
        per = TILE // ROWS
        attend_rows(blocks_of(qa, t * per, per), long_keys, LONG_KEYS // CHUNK, pl.ds(t * per, per))

    def short_keys(c):
        at = LONG + c * per_chunk
        docs = [doc_ref[packed(at + b)] for b in range(per_chunk)]
        return blocks_of(ka, at, per_chunk), blocks_of(va, at, per_chunk), docs

    def short_tile(t):
        per = SHORT_TILE // ROWS
        at = LONG + t * per
        docs = jnp.concatenate([jnp.full((ROWS, 128), doc_ref[packed(at + b)], jnp.int32) for b in range(per)], axis=0)
        attend_rows(blocks_of(qa, at, per), short_keys, SHORT_KEYS // CHUNK, pl.ds(at, per), docs)

    loop((BLOCKS - LONG) * ROWS // SHORT_TILE, short_tile)
    loop(LONG * ROWS // TILE, long_tile)

    whole = o_ref[...].astype(F32).reshape(BLOCKS, 4, PIECE, 128)
    square = jnp.sum(whole * whole, axis=1).reshape(BLOCKS * PIECE, 128)
    high = square.astype(BF16)
    low = (square - high.astype(F32)).astype(BF16)
    ones = jnp.ones((8, 128), BF16)
    dims = (((1,), (1,)), ((), ()))
    sq_out[...] = lax.dot_general(ones, high, dims, preferred_element_type=F32) + lax.dot_general(
        ones, low, dims, preferred_element_type=F32
    )

    me8 = me.plane * 4 + me.kv
    home_core = me.kv // 2
    half = me.kv % 2

    def partners(src, box, s_sem, r_sem, run):
        def one(i):
            @pl.when(i != me8)
            def _():
                device = me.at(i % 4 + 4 * (me.z // 4), me.y, me.core, i // 4)
                run(send(src, box.at[me8], s_sem.at[i], r_sem.at[me8], device))

        loop(8, one)

    def from_partners(box, r_sem):
        def one(i):
            @pl.when(i != me8)
            def _():
                arrived(box.at[i], r_sem.at[i])

        loop(8, one)

    start = lambda copy: copy.start()
    sent = lambda copy: copy.wait_send()

    partners(sq_out, sq_in, s_sq, r_sq, start)
    sq_in[me8] = sq_out[...]

    def result(j, run):
        s = (j + me.ctx) % 32
        src = res.at[pl.ds(2 * s, 2)]
        slot = half * 16 + me.piece
        run(
            me.is_me(s // 4, s % 4, home_core),
            send(src, home.at[slot], s_o.at[s], r_o.at[slot], me.at(s // 4, s % 4, home_core)),
            pltpu.make_async_copy(src, home.at[slot], r_o.at[slot]),
        )

    def move(p):
        res[p] = o_ref[sorted_place(source_ref[p])]

    loop(BLOCKS, move)
    def results_out(first_one, count):
        loop(count, lambda j: result(first_one + j, start_either))

    results_out(0, OUT_1)

    lat = lat_in[...]
    gained = []
    for h in range(4):
        part = whole[:, h].reshape(BLOCKS * PIECE, 128)
        gained.append((part * gain_in[h : h + 1, :]).astype(BF16))
    gained = jnp.concatenate(gained, axis=1)
    s = lax.dot_general(lat, gained, (((1,), (1,)), ((), ())), preferred_element_type=F32)
    tokens = lax.broadcasted_iota(jnp.int32, (DOCS, PIECE), 0)
    hot = jnp.concatenate(
        [(tokens == doc_ref[packed(i)]).astype(F32) for i in range(BLOCKS)], axis=1
    ).astype(BF16)
    sends_done()
    from_partners(sq_in, r_sq)
    channel_total = jnp.sum(sq_in[...], axis=0)
    factor = lax.rsqrt(channel_total / CHANNELS + EPS) * (math.log2(math.e) * 512 ** (-0.5))
    s = s.reshape(64, 8, BLOCKS * PIECE) * factor[None]
    top = jnp.max(jnp.max(s, axis=0), axis=0, keepdims=True)
    w = jnp.exp2(s - top[None])
    w = w * (1.0 / jnp.sum(jnp.sum(w, axis=0), axis=0, keepdims=True))[None]
    w = w.reshape(512, BLOCKS * PIECE).astype(BF16)
    by_doc = lax.dot_general(hot, w, (((1,), (1,)), ((), ())), preferred_element_type=F32)
    sums = None
    for _ in range(3):
        part = by_doc.astype(BF16)
        by_doc = by_doc - part.astype(F32)
        add = jnp.dot(part, lat, preferred_element_type=F32)
        sums = add if sums is None else sums + add

    w8 = me.piece % 8
    doc_out[...] = jnp.concatenate(
        [
            sums[two * 8 : two * 8 + 8, h * 128 : h * 128 + 128].reshape(8, 1, 128)
            for two in range(2)
            for h in range(4)
        ],
        axis=1,
    )

    def document(w, run):
        run(
            w == w8,
            send(doc_out.at[w], doc_in.at[w8], s_d.at[w], r_d.at[w8], me.at(me.z, w // 2, w % 2)),
            pltpu.make_async_copy(doc_out.at[w], doc_in.at[w8], r_d.at[w8]),
        )

    loop(8, lambda w: document(w, start_either))
    results_out(OUT_1, OUT_2)
    loop(8, lambda w: arrived(doc_in.at[w], r_d.at[w]))
    row_out[...] = jnp.sum(doc_in[...], axis=0)

    def share(j, run):
        s = (j + me.ctx) % 32
        dst = row_in.at[half, me.piece]
        slot = half * 16 + me.piece
        run(
            me.is_me(s // 4, s % 4, home_core),
            send(row_out, dst, s_e.at[s], r_e.at[slot], me.at(s // 4, s % 4, home_core)),
            pltpu.make_async_copy(row_out, dst, r_e.at[slot]),
        )

    loop(32, lambda j: share(j, start_either))
    results_out(OUT_1 + OUT_2, 32 - OUT_1 - OUT_2)

    loop(32, lambda i: arrived(home.at[i], r_o.at[i]))
    for side in range(2):
        for block in range(2):
            for pair in range(8):
                rows = []
                for part in range(2):
                    piece = home[side * 16 + pair * 2 + part, block].astype(F32)
                    rows.append(jnp.concatenate([piece[h * 8 : h * 8 + 8] for h in range(4)], axis=1))
                at = block * BLOCK + pair * 16
                att_ref[at : at + 16, side * 512 : side * 512 + 512] = jnp.concatenate(rows, axis=0).astype(BF16)

    loop(32, lambda i: arrived(row_in.at[i // 16, i % 16], r_e.at[i]))
    rows = row_in[...]
    rows = rows[:, 0:8] + rows[:, 8:16]
    for two in range(2):
        square = rows[:, :, two * 4 : two * 4 + 4, :]
        square = jnp.sum(square * square, axis=(0, 2))
        norm_out[two] = jnp.broadcast_to(jnp.sum(square, axis=-1, keepdims=True), (8, 128))
    my_head = me.plane * 2 + core

    def head(i, run):
        @pl.when(i != my_head)
        def _():
            device = me.at(me.z, me.y, i % 2, i // 2)
            run(send(norm_out, norm_in.at[my_head], s_n.at[i], r_n.at[my_head], device))

    loop(4, lambda i: head(i, start))
    norm_in[my_head] = norm_out[...]

    def from_head(i):
        @pl.when(i != my_head)
        def _():
            arrived(norm_in.at[i], r_n.at[i])

    loop(4, from_head)
    factors = lax.rsqrt(jnp.sum(norm_in[...], axis=0) / CHANNELS + EPS)
    for side in range(2):
        for h in range(4):
            at = side * 512 + h * 128
            for two in range(2):
                emb_ref[two * 8 : two * 8 + 8, at : at + 128] = rows[side, :, two * 4 + h, :] * factors[two]

    partners(sq_out, sq_in, s_sq, r_sq, sent)
    loop(4, lambda i: head(i, sent))
    loop(32, lambda j: result(j, end_either))
    loop(8, lambda w: document(w, end_either))
    loop(32, lambda j: share(j, end_either))


def shards(queries, keys, values, latents, norm_gain, block_doc, block_source):
    dma = pltpu.SemaphoreType.DMA
    hbm = pl.BlockSpec(memory_space=pltpu.HBM)
    vmem = pl.BlockSpec(memory_space=pltpu.VMEM)
    smem = pl.BlockSpec(memory_space=pltpu.SMEM)
    tokens = BLOCKS * BLOCK
    return pl.pallas_call(
        kernel,
        out_shape=(
            jax.ShapeDtypeStruct((256, 1024), BF16),
            jax.ShapeDtypeStruct((DOCS, 1024), F32),
        ),
        in_specs=[smem, smem] + [hbm] * 5,
        out_specs=(vmem, vmem),
        scratch_shapes=[
            pltpu.VMEM((2, BLOCK, 1024), BF16),
            pltpu.VMEM((32, 2 * ROWS, HEAD_DIM), BF16),
            pltpu.VMEM((32, 2 * ROWS, HEAD_DIM), BF16),
            pltpu.VMEM((2, tokens, HEAD_DIM), BF16),
            pltpu.VMEM((512, 512), BF16),
            pltpu.VMEM((4, 128), F32),
            pltpu.VMEM((BLOCKS, BLOCK, 256), BF16),
            pltpu.VMEM((BLOCKS, BLOCK, 256), BF16),
            pltpu.VMEM((BLOCKS, ROWS, 256), BF16),
            pltpu.VMEM((BLOCKS, ROWS, HEAD_DIM), BF16),
            pltpu.VMEM((BLOCKS, ROWS, HEAD_DIM), BF16),
            pltpu.VMEM((32, 2, ROWS, HEAD_DIM), BF16),
            pltpu.VMEM((8, BLOCKS * PIECE), F32),
            pltpu.VMEM((8, 8, BLOCKS * PIECE), F32),
            pltpu.VMEM((8, 8, 128), F32),
            pltpu.VMEM((8, 8, 128), F32),
            pltpu.VMEM((2, 8, 128), F32),
            pltpu.VMEM((4, 2, 8, 128), F32),
            pltpu.VMEM((8, 128), F32),
            pltpu.VMEM((2, 16, 8, 128), F32),
            dma((PARTS, 2, 8)), dma((PARTS, 8)),
            dma((2, PARTS, 8)), dma((2, PARTS, 8)),
            dma((2, PARTS, 8)), dma((2, PARTS, 8)),
            dma((8,)), dma((8,)),
            dma((32,)), dma((32,)),
            dma((2,)), dma((2,)),
            dma,
            dma((32,)), dma((32,)),
            dma((8,)), dma((8,)),
            dma((8,)), dma((8,)),
            dma((4,)), dma((4,)),
            dma((32,)), dma((32,)),
        ],
        compiler_params=pltpu.CompilerParams(
            collective_id=0, has_side_effects=True, vmem_limit_bytes=60 * 1024 * 1024
        ),
        name="embed",
    )(
        block_doc, block_source, queries.reshape(2, BLOCK, 1024), keys, values, latents, norm_gain.reshape(2, 4, 128)
    )


def solution(mesh):
    in_specs = (
        P(("dp", "ctx"), "head"),
        P(("dp", "ctx"), "head"),
        P(("dp", "ctx"), "head"),
        P(None, "head"),
        P("head"),
        P("dp"),
        P("dp"),
    )
    out_specs = (P(("dp", "ctx"), "head"), P("dp", "head"))
    return jax.shard_map(shards, mesh=mesh, in_specs=in_specs, out_specs=out_specs, check_vma=False)
```

```python
import functools
import math

import jax
import jax.numpy as jnp
from jax import lax
from jax.experimental import pallas as pl
from jax.experimental.pallas import tpu as pltpu
from jax.sharding import PartitionSpec as P

HEADS = 32
HEAD_DIM = 128
BLOCK = 128
BLOCKS = 64
LONG = 40
DOCS = 16
CHANNELS = HEADS * HEAD_DIM
PIECE = 8
ROWS = 4 * PIECE
TILE = 1280
SHORT_TILE = 384
CHUNK = 256
LONG_KEYS = LONG * BLOCK
SHORT_KEYS = (BLOCKS - LONG) * BLOCK
EPS = 1e-05
PARTS = 1
PART = 256 // PARTS
HALF = PART // 2
AHEAD = 4
LAY = 2
Q_START = 4
Q_STEP = 4
LAG = 4
MESH = pl.DeviceIdType.MESH
F32 = jnp.float32
BF16 = jnp.bfloat16


def loop(count, body):
    def step(i, carry):
        body(i)
        return carry

    lax.fori_loop(0, count, step, 0)


class Place:
    def __init__(self):
        self.ctx = lax.axis_index("ctx")
        head = lax.axis_index("head")
        self.z = self.ctx // 4
        self.y = self.ctx % 4
        self.plane = head // 2
        self.core = head % 2
        self.kv = self.z % 4
        self.piece = (self.z // 4) * 8 + self.y * 2 + self.core

    def at(self, z, y, core, plane=None):
        plane = self.plane if plane is None else plane
        return {"ctx": z * 4 + y, "head": plane * 2 + core}

    def worker(self, kv, piece):
        return (kv + 4 * (piece // 8), (piece % 8) // 2, piece % 2)

    def far(self, j):
        k, i = j // 4, j % 4
        dz = 4 + (k % 2) * ((k + 1) // 2) - (1 - k % 2) * (k // 2)
        dy = 2 + (i % 2) * ((i + 1) // 2) - (1 - i % 2) * (i // 2)
        return (self.z + dz) % 8, (self.y + dy) % 4

    def is_me(self, z, y, core):
        return (z == self.z) & (y == self.y) & (core == self.core)


def greet(me):
    barrier = pltpu.get_barrier_semaphore()

    def one(i):
        z, y = me.far(i // 2)
        core = i % 2

        @pl.when(jnp.logical_not(me.is_me(z, y, core)))
        def _():
            pl.semaphore_signal(barrier, 1, device_id=me.at(z, y, core), device_id_type=MESH)

    def other(i):
        here = i == 4
        z = jnp.where(here, me.z, i % 4 + 4 * (me.z // 4))
        core = jnp.where(here, 1 - me.core, me.core)
        pl.semaphore_signal(barrier, 1, device_id=me.at(z, me.y, core, 1 - me.plane), device_id_type=MESH)

    loop(64, one)
    loop(5, other)
    return barrier


def send(src, dst, send_sem, recv_sem, device):
    return pltpu.make_async_remote_copy(
        src_ref=src, dst_ref=dst, send_sem=send_sem, recv_sem=recv_sem, device_id=device, device_id_type=MESH
    )


def arrived(ref, sem):
    pltpu.make_async_copy(ref, ref, sem).wait()


def start_either(here, remote, local):
    @pl.when(here)
    def _():
        local.start()

    @pl.when(jnp.logical_not(here))
    def _():
        remote.start()


def end_either(here, remote, local):
    @pl.when(jnp.logical_not(here))
    def _():
        remote.wait_send()


def kernel(
    doc_ref, source_ref, q_ref, k_ref, v_ref, lat_ref, gain_ref,
    att_ref, emb_ref,
    q_in, qs, qp, kv, lat_in, gain_in, ka, va, qa, o_ref, res,
    home, sq_out, sq_in, doc_out, doc_in, norm_out, norm_in, row_out, row_in,
    s_a, r_a, s_b, r_b, s_c, r_c, s_s, r_s, s_q, r_q, s_l, r_l, l_q,
    s_o, r_o, s_sq, r_sq, s_d, r_d, s_n, r_n, s_e, r_e,
    att, l_att,
):
    me = Place()
    z, y, core = me.z, me.y, me.core
    load_q = pltpu.make_async_copy(q_ref, q_in, l_q)
    load_q.start()
    barrier = greet(me)

    load_q.wait()

    def regroup(i):
        half, pair = i // 8, i % 8
        rows_at = pl.ds(pl.multiple_of(pair * 16, 16), 16)
        for block in range(2):
            tile = q_in[block, rows_at, pl.ds(pl.multiple_of(half * 512, 512), 512)].astype(F32)
            for part in range(2):
                rows = tile[part * 8 : part * 8 + 8]
                rows = jnp.concatenate([rows[:, h * 128 : h * 128 + 128] for h in range(4)], axis=0)
                qs[2 * i + part, block * ROWS : block * ROWS + ROWS, :] = rows.astype(BF16)

    loop(16, regroup)
    va[:, :, 128:256] = jnp.ones((BLOCKS, BLOCK, 128), BF16)

    first = jnp.int32(0)
    for i in range(BLOCKS - LONG + 1):
        first = jnp.where(doc_ref[i] == doc_ref[i + LONG - 1], i, first)

    def packed(i):
        return jnp.where(i < LONG, first + i, jnp.where(i - LONG < first, i - LONG, i))

    def sorted_place(at):
        return jnp.where(at < first, at + LONG, jnp.where(at < first + LONG, at - first, at))

    pl.semaphore_wait(barrier, 68)

    up, down = (y + 1) % 4, (y + 3) % 4
    mine = me.kv // 2 == core

    def order(j):
        odd = j % 2
        return odd * ((j + 1) // 2) + (1 - odd) * (8 - j // 2)

    def column(j, run):
        to_z = (z + order(j)) % 8

        @pl.when((to_z % 4) // 2 == core)
        def _():
            half = to_z % 2
            for part in range(PARTS):
                for kind in range(2):
                    first = part * PART
                    columns = pl.ds(pl.multiple_of(half * HEAD_DIM, HEAD_DIM), HEAD_DIM)
                    src = (k_ref, v_ref)[kind].at[pl.ds(first, PART), columns]
                    dst = kv.at[kind, pl.ds(pl.multiple_of(me.ctx * 256 + first, PART), PART), :]
                    sem = r_a.at[part, z]
                    here = (to_z == z) & (core == kind)
                    copy = send(src, dst, s_a.at[part, kind, to_z], sem, me.at(to_z, y, kind))
                    run(here, copy, pltpu.make_async_copy(src, dst, sem))

    loop(AHEAD, lambda j: column(j, start_either))

    def query(j, run):
        i = (j + me.ctx) % 32
        to = me.worker(2 * core + i // 16, i % 16)
        run(
            me.is_me(*to),
            send(qs.at[i], qp.at[me.ctx], s_q.at[i], r_q.at[me.ctx], me.at(*to)),
            pltpu.make_async_copy(qs.at[i], qp.at[me.ctx], r_q.at[me.ctx]),
        )

    def rows_of(from_z, from_y, first=0, count=256):
        start = pl.multiple_of((from_z * 4 + from_y) * 256 + first, HALF)
        return kv.at[core, pl.ds(start, count), :]

    def to_core(from_z):
        rows = kv.at[core, pl.ds(pl.multiple_of(from_z * 1024, 1024), 1024), :]
        return send(rows, rows, s_s.at[from_z], r_s.at[from_z], me.at(z, y, 1 - core))

    def near(from_z, part):
        rows = rows_of(from_z, y, part * PART, PART)
        return (
            send(rows, rows, s_b.at[0, part, from_z], r_b.at[0, part, from_z], me.at(z, up, core)),
            send(rows, rows, s_b.at[1, part, from_z], r_b.at[1, part, from_z], me.at(z, down, core)),
        )

    def onward(from_z, part):
        one = rows_of(from_z, down, part * PART, HALF)
        two = rows_of(from_z, up, part * PART + HALF, HALF)
        return (
            send(one, one, s_c.at[0, part, from_z], r_c.at[0, part, from_z], me.at(z, up, core)),
            send(two, two, s_c.at[1, part, from_z], r_c.at[1, part, from_z], me.at(z, down, core)),
        )

    steps = 8 * PARTS

    def at_step(e):
        return (z + order(e // PARTS)) % 8, e % PARTS

    def arrange_keys(j):
        from_z = (z + order(j)) % 8
        rows = pl.ds(pl.multiple_of(from_z * 1024, 1024), 1024)
        blocks = pl.ds(from_z * 8, 8)
        arrived(kv.at[1 - core, rows, :], r_s.at[from_z])
        key = kv[0, rows, :].reshape(8, BLOCK, 128)
        ka[blocks, :, 0:128] = key
        ka[blocks, :, 128:256] = key
        va[blocks, :, 0:128] = kv[1, rows, :].reshape(8, BLOCK, 128)

    def ring(e):
        @pl.when(e < steps)
        def _():
            @pl.when((e % PARTS == 0) & (e // PARTS + AHEAD < 8))
            def _():
                column(e // PARTS + AHEAD, start_either)

            from_z, part = at_step(e)
            arrived(rows_of(from_z, y, part * PART, PART), r_a.at[part, from_z])
            for copy in near(from_z, part):
                copy.start()

        @pl.when((e >= Q_START) & (e < Q_START + 32 // Q_STEP))
        def _():
            for i in range(Q_STEP):
                query((e - Q_START) * Q_STEP + i, start_either)

        @pl.when((e >= LAG) & (e < steps + LAG))
        def _():
            from_z, part = at_step(e - LAG)
            copies = onward(from_z, part)
            arrived(rows_of(from_z, down, part * PART, PART), r_b.at[0, part, from_z])
            copies[0].start()
            arrived(rows_of(from_z, up, part * PART, PART), r_b.at[1, part, from_z])
            copies[1].start()

        @pl.when(e >= 2 * LAG)
        def _():
            from_z, part = at_step(e - 2 * LAG)
            opposite = (y + 2) % 4
            arrived(rows_of(from_z, opposite, part * PART, HALF), r_c.at[0, part, from_z])
            arrived(rows_of(from_z, opposite, part * PART + HALF, HALF), r_c.at[1, part, from_z])

            @pl.when(part == PARTS - 1)
            def _():
                to_core(from_z).start()

        @pl.when(e >= 2 * LAG + LAY)
        def _():
            arrange_keys(e - 2 * LAG - LAY)

    loop(steps + 2 * LAG, ring)

    def pool_inputs():
        other = me.at(z, y, 1 - core)
        half = me.kv % 2
        lat = lat_ref.at[:, pl.ds(pl.multiple_of(half * 512, 512), 512)]
        gain = gain_ref.at[half]
        return (
            pltpu.make_async_copy(lat, lat_in, r_l.at[0]),
            pltpu.make_async_copy(gain, gain_in, r_l.at[1]),
            send(lat, lat_in, s_l.at[0], r_l.at[0], other),
            send(gain, gain_in, s_l.at[1], r_l.at[1], other),
        )

    @pl.when(mine)
    def _():
        for copy in pool_inputs():
            copy.start()

    def sends_done():
        loop(8, lambda j: column(j, end_either))

        def ring_done(e):
            from_z, part = at_step(e)
            for copy in near(from_z, part) + onward(from_z, part):
                copy.wait_send()

        loop(steps, ring_done)
        loop(32, lambda j: query(j, end_either))
        loop(8, lambda from_z: to_core(from_z).wait_send())

        @pl.when(mine)
        def _():
            for copy in pool_inputs()[2:]:
                copy.wait_send()

    scale = math.log2(math.e) * HEAD_DIM ** (-0.5)

    def arrange_queries(s):
        arrived(qp.at[s], r_q.at[s])
        query = qp[s].reshape(2, ROWS, 128).astype(F32) * scale
        high = query.astype(BF16)
        blocks = pl.ds(2 * s, 2)
        qa[blocks, :, 0:128] = high
        qa[blocks, :, 128:256] = (query - high.astype(F32)).astype(BF16)

    loop(32, arrange_queries)
    loop(LAY, lambda j: arrange_keys(8 - LAY + j))

    for copy in pool_inputs()[:2]:
        copy.wait()

    def blocks_of(ref, first_block, count):
        return jnp.concatenate([ref[packed(first_block + b)] for b in range(count)], axis=0)

    def attend_rows(q, keys_at, chunks, rows, docs=None):
        m = total = None
        for c in range(chunks):
            key, value, key_docs = keys_at(c)
            s = lax.dot_general(q, key, (((1,), (1,)), ((), ())), preferred_element_type=F32)
            parts = [s[:, b * 128 : b * 128 + 128] for b in range(CHUNK // 128)]
            if docs is not None:
                parts = [jnp.where(docs == doc, part, -1e30) for doc, part in zip(key_docs, parts)]
            top = functools.reduce(jnp.maximum, parts)
            top = jnp.broadcast_to(jnp.max(top, axis=1, keepdims=True), top.shape)
            new_m = top if m is None else jnp.maximum(m, top)
            w = jnp.concatenate([jnp.exp2(part - new_m).astype(BF16) for part in parts], axis=1)
            add = jnp.dot(w, value, preferred_element_type=F32)
            if m is None:
                total = add
            else:
                shrink = jnp.exp2(m - new_m)
                total = total * jnp.concatenate([shrink, shrink], axis=1) + add
            m = new_m
        o_ref[rows] = (total[:, 0:128] / total[:, 128:256]).astype(BF16).reshape(-1, ROWS, 128)

    per_chunk = CHUNK // BLOCK

    def long_keys(c):
        return blocks_of(ka, c * per_chunk, per_chunk), blocks_of(va, c * per_chunk, per_chunk), None

    def long_tile(t):
        per = TILE // ROWS
        attend_rows(blocks_of(qa, t * per, per), long_keys, LONG_KEYS // CHUNK, pl.ds(t * per, per))

    def short_keys(c):
        at = LONG + c * per_chunk
        docs = [doc_ref[packed(at + b)] for b in range(per_chunk)]
        return blocks_of(ka, at, per_chunk), blocks_of(va, at, per_chunk), docs

    def short_tile(t):
        per = SHORT_TILE // ROWS
        at = LONG + t * per
        docs = jnp.concatenate([jnp.full((ROWS, 128), doc_ref[packed(at + b)], jnp.int32) for b in range(per)], axis=0)
        attend_rows(blocks_of(qa, at, per), short_keys, SHORT_KEYS // CHUNK, pl.ds(at, per), docs)

    loop((BLOCKS - LONG) * ROWS // SHORT_TILE, short_tile)
    loop(LONG * ROWS // TILE, long_tile)

    whole = o_ref[...].astype(F32).reshape(BLOCKS, 4, PIECE, 128)
    square = jnp.sum(whole * whole, axis=1).reshape(BLOCKS * PIECE, 128)
    high = square.astype(BF16)
    low = (square - high.astype(F32)).astype(BF16)
    ones = jnp.ones((8, 128), BF16)
    dims = (((1,), (1,)), ((), ()))
    sq_out[...] = lax.dot_general(ones, high, dims, preferred_element_type=F32) + lax.dot_general(
        ones, low, dims, preferred_element_type=F32
    )

    me8 = me.plane * 4 + me.kv
    home_core = me.kv // 2
    half = me.kv % 2

    def partners(src, box, s_sem, r_sem, run):
        def one(i):
            @pl.when(i != me8)
            def _():
                device = me.at(i % 4 + 4 * (me.z // 4), me.y, me.core, i // 4)
                run(send(src, box.at[me8], s_sem.at[i], r_sem.at[me8], device))

        loop(8, one)

    def from_partners(box, r_sem):
        def one(i):
            @pl.when(i != me8)
            def _():
                arrived(box.at[i], r_sem.at[i])

        loop(8, one)

    start = lambda copy: copy.start()
    sent = lambda copy: copy.wait_send()

    partners(sq_out, sq_in, s_sq, r_sq, start)
    sq_in[me8] = sq_out[...]

    def result(j, run):
        s = (j + me.ctx) % 32
        src = res.at[pl.ds(2 * s, 2)]
        slot = half * 16 + me.piece
        run(
            me.is_me(s // 4, s % 4, home_core),
            send(src, home.at[slot], s_o.at[s], r_o.at[slot], me.at(s // 4, s % 4, home_core)),
            pltpu.make_async_copy(src, home.at[slot], r_o.at[slot]),
        )

    def move(p):
        res[p] = o_ref[sorted_place(source_ref[p])]

    loop(BLOCKS, move)
    loop(32, lambda j: result(j, start_either))

    lat = lat_in[...]
    gained = []
    for h in range(4):
        part = whole[:, h].reshape(BLOCKS * PIECE, 128)
        gained.append((part * gain_in[h : h + 1, :]).astype(BF16))
    gained = jnp.concatenate(gained, axis=1)
    s = lax.dot_general(lat, gained, (((1,), (1,)), ((), ())), preferred_element_type=F32)
    tokens = lax.broadcasted_iota(jnp.int32, (DOCS, PIECE), 0)
    hot = jnp.concatenate(
        [(tokens == doc_ref[packed(i)]).astype(F32) for i in range(BLOCKS)], axis=1
    ).astype(BF16)
    from_partners(sq_in, r_sq)
    channel_total = jnp.sum(sq_in[...], axis=0)
    factor = lax.rsqrt(channel_total / CHANNELS + EPS) * (math.log2(math.e) * 512 ** (-0.5))
    s = s.reshape(64, 8, BLOCKS * PIECE) * factor[None]
    top = jnp.max(jnp.max(s, axis=0), axis=0, keepdims=True)
    w = jnp.exp2(s - top[None])
    w = w * (1.0 / jnp.sum(jnp.sum(w, axis=0), axis=0, keepdims=True))[None]
    w = w.reshape(512, BLOCKS * PIECE).astype(BF16)
    by_doc = lax.dot_general(hot, w, (((1,), (1,)), ((), ())), preferred_element_type=F32)
    sums = None
    for _ in range(3):
        part = by_doc.astype(BF16)
        by_doc = by_doc - part.astype(F32)
        add = jnp.dot(part, lat, preferred_element_type=F32)
        sums = add if sums is None else sums + add

    w8 = me.piece % 8
    doc_out[...] = jnp.concatenate(
        [
            sums[two * 8 : two * 8 + 8, h * 128 : h * 128 + 128].reshape(8, 1, 128)
            for two in range(2)
            for h in range(4)
        ],
        axis=1,
    )

    def document(w, run):
        run(
            w == w8,
            send(doc_out.at[w], doc_in.at[w8], s_d.at[w], r_d.at[w8], me.at(me.z, w // 2, w % 2)),
            pltpu.make_async_copy(doc_out.at[w], doc_in.at[w8], r_d.at[w8]),
        )

    loop(8, lambda w: document(w, start_either))
    loop(8, lambda w: arrived(doc_in.at[w], r_d.at[w]))
    row_out[...] = jnp.sum(doc_in[...], axis=0)

    def share(j, run):
        to_z, to_y = me.far(j)
        dst = row_in.at[half, me.piece]
        slot = half * 16 + me.piece
        run(
            me.is_me(to_z, to_y, home_core),
            send(row_out, dst, s_e.at[j], r_e.at[slot], me.at(to_z, to_y, home_core)),
            pltpu.make_async_copy(row_out, dst, r_e.at[slot]),
        )

    loop(32, lambda j: share(j, start_either))
    sends_done()

    loop(32, lambda i: arrived(home.at[i], r_o.at[i]))
    for side in range(2):
        for block in range(2):
            for pair in range(8):
                rows = []
                for part in range(2):
                    piece = home[side * 16 + pair * 2 + part, block].astype(F32)
                    rows.append(jnp.concatenate([piece[h * 8 : h * 8 + 8] for h in range(4)], axis=1))
                at = block * BLOCK + pair * 16
                att[at : at + 16, side * 512 : side * 512 + 512] = jnp.concatenate(rows, axis=0).astype(BF16)
    att_out = pltpu.make_async_copy(att, att_ref, l_att)
    att_out.start()

    loop(32, lambda i: arrived(row_in.at[i // 16, i % 16], r_e.at[i]))
    rows = row_in[...]
    rows = rows[:, 0:8] + rows[:, 8:16]
    for two in range(2):
        square = rows[:, :, two * 4 : two * 4 + 4, :]
        square = jnp.sum(square * square, axis=(0, 2))
        norm_out[two] = jnp.broadcast_to(jnp.sum(square, axis=-1, keepdims=True), (8, 128))
    my_head = me.plane * 2 + core

    def head(i, run):
        @pl.when(i != my_head)
        def _():
            device = me.at(me.z, me.y, i % 2, i // 2)
            run(send(norm_out, norm_in.at[my_head], s_n.at[i], r_n.at[my_head], device))

    loop(4, lambda i: head(i, start))
    norm_in[my_head] = norm_out[...]

    def from_head(i):
        @pl.when(i != my_head)
        def _():
            arrived(norm_in.at[i], r_n.at[i])

    partners(sq_out, sq_in, s_sq, r_sq, sent)
    loop(32, lambda j: result(j, end_either))
    loop(8, lambda w: document(w, end_either))
    loop(32, lambda j: share(j, end_either))
    loop(4, lambda i: head(i, sent))
    loop(4, from_head)
    factors = lax.rsqrt(jnp.sum(norm_in[...], axis=0) / CHANNELS + EPS)
    for side in range(2):
        for h in range(4):
            at = side * 512 + h * 128
            for two in range(2):
                emb_ref[two * 8 : two * 8 + 8, at : at + 128] = rows[side, :, two * 4 + h, :] * factors[two]
    att_out.wait()


def shards(queries, keys, values, latents, norm_gain, block_doc, block_source):
    dma = pltpu.SemaphoreType.DMA
    hbm = pl.BlockSpec(memory_space=pltpu.HBM)
    vmem = pl.BlockSpec(memory_space=pltpu.VMEM)
    smem = pl.BlockSpec(memory_space=pltpu.SMEM)
    tokens = BLOCKS * BLOCK
    outs = pl.pallas_call(
        kernel,
        out_shape=(
            jax.ShapeDtypeStruct((256, 1024), BF16),
            jax.ShapeDtypeStruct((DOCS, 1024), F32),
        ),
        in_specs=[smem, smem] + [hbm] * 5,
        out_specs=(hbm, vmem),
        scratch_shapes=[
            pltpu.VMEM((2, BLOCK, 1024), BF16),
            pltpu.VMEM((32, 2 * ROWS, HEAD_DIM), BF16),
            pltpu.VMEM((32, 2 * ROWS, HEAD_DIM), BF16),
            pltpu.VMEM((2, tokens, HEAD_DIM), BF16),
            pltpu.VMEM((512, 512), BF16),
            pltpu.VMEM((4, 128), F32),
            pltpu.VMEM((BLOCKS, BLOCK, 256), BF16),
            pltpu.VMEM((BLOCKS, BLOCK, 256), BF16),
            pltpu.VMEM((BLOCKS, ROWS, 256), BF16),
            pltpu.VMEM((BLOCKS, ROWS, HEAD_DIM), BF16),
            pltpu.VMEM((BLOCKS, ROWS, HEAD_DIM), BF16),
            pltpu.VMEM((32, 2, ROWS, HEAD_DIM), BF16),
            pltpu.VMEM((8, BLOCKS * PIECE), F32),
            pltpu.VMEM((8, 8, BLOCKS * PIECE), F32),
            pltpu.VMEM((8, 8, 128), F32),
            pltpu.VMEM((8, 8, 128), F32),
            pltpu.VMEM((2, 8, 128), F32),
            pltpu.VMEM((4, 2, 8, 128), F32),
            pltpu.VMEM((8, 128), F32),
            pltpu.VMEM((2, 16, 8, 128), F32),
            dma((PARTS, 2, 8)), dma((PARTS, 8)),
            dma((2, PARTS, 8)), dma((2, PARTS, 8)),
            dma((2, PARTS, 8)), dma((2, PARTS, 8)),
            dma((8,)), dma((8,)),
            dma((32,)), dma((32,)),
            dma((2,)), dma((2,)),
            dma,
            dma((32,)), dma((32,)),
            dma((8,)), dma((8,)),
            dma((8,)), dma((8,)),
            dma((4,)), dma((4,)),
            dma((32,)), dma((32,)),
            pltpu.VMEM((256, 1024), BF16),
            dma,
        ],
        compiler_params=pltpu.CompilerParams(
            collective_id=0, has_side_effects=True, vmem_limit_bytes=60 * 1024 * 1024
        ),
        name="embed",
    )(
        block_doc, block_source, queries.reshape(2, BLOCK, 1024), keys, values, latents, norm_gain.reshape(2, 4, 128)
    )
    return written(*outs)


def out_kernel(att_ref, emb_ref, att_out, emb_out, att, emb, sems_in, sems_out):
    pieces = [(emb_ref, emb, emb_out)]
    for i in range(4):
        rows = pl.ds(64 * i, 64)
        pieces.append((att_ref.at[rows], att.at[rows], att_out.at[rows]))
    into = [pltpu.make_async_copy(src, held, sems_in.at[i]) for i, (src, held, _) in enumerate(pieces)]
    out = [pltpu.make_async_copy(held, dst, sems_out.at[i]) for i, (_, held, dst) in enumerate(pieces)]
    for copy in into:
        copy.start()
    for one, two in zip(into, out):
        one.wait()
        two.start()
    for copy in out:
        copy.wait()


def written(attended, embeddings):
    hbm = pl.BlockSpec(memory_space=pltpu.HBM)
    return pl.pallas_call(
        out_kernel,
        out_shape=(
            jax.ShapeDtypeStruct(attended.shape, attended.dtype),
            jax.ShapeDtypeStruct(embeddings.shape, embeddings.dtype),
        ),
        in_specs=[hbm, hbm],
        out_specs=(hbm, hbm),
        scratch_shapes=[
            pltpu.VMEM(attended.shape, attended.dtype),
            pltpu.VMEM(embeddings.shape, embeddings.dtype),
            pltpu.SemaphoreType.DMA((5,)),
            pltpu.SemaphoreType.DMA((5,)),
        ],
        compiler_params=pltpu.CompilerParams(vmem_limit_bytes=60 * 1024 * 1024),
        name="written",
    )(attended, embeddings)


def solution(mesh):
    in_specs = (
        P(("dp", "ctx"), "head"),
        P(("dp", "ctx"), "head"),
        P(("dp", "ctx"), "head"),
        P(None, "head"),
        P("head"),
        P("dp"),
        P("dp"),
    )
    out_specs = (P(("dp", "ctx"), "head"), P("dp", "head"))
    return jax.shard_map(shards, mesh=mesh, in_specs=in_specs, out_specs=out_specs, check_vma=False)
```

```python
import functools
import math

import jax
import jax.numpy as jnp
from jax import lax
from jax.experimental import pallas as pl
from jax.experimental.pallas import tpu as pltpu
from jax.sharding import PartitionSpec as P

HEADS = 32
HEAD_DIM = 128
BLOCK = 128
BLOCKS = 64
LONG = 40
DOCS = 16
CHANNELS = HEADS * HEAD_DIM
PIECE = 8
ROWS = 4 * PIECE
TILE = 1280
SHORT_TILE = 256
CHUNK = 256
LONG_KEYS = LONG * BLOCK
SHORT_KEYS = (BLOCKS - LONG) * BLOCK
EPS = 1e-05
PARTS = 1
PART = 256 // PARTS
HALF = PART // 2
AHEAD = 4
LAY = 2
Q_START = 4
Q_STEP = 4
LAG = 4
MESH = pl.DeviceIdType.MESH
F32 = jnp.float32
BF16 = jnp.bfloat16


def loop(count, body):
    def step(i, carry):
        body(i)
        return carry

    lax.fori_loop(0, count, step, 0)


class Place:
    def __init__(self):
        self.ctx = lax.axis_index("ctx")
        head = lax.axis_index("head")
        self.z = self.ctx // 4
        self.y = self.ctx % 4
        self.plane = head // 2
        self.core = head % 2
        self.kv = self.z % 4
        self.piece = (self.z // 4) * 8 + self.y * 2 + self.core

    def at(self, z, y, core, plane=None):
        plane = self.plane if plane is None else plane
        return {"ctx": z * 4 + y, "head": plane * 2 + core}

    def worker(self, kv, piece):
        return (kv + 4 * (piece // 8), (piece % 8) // 2, piece % 2)

    def far(self, j):
        k, i = j // 4, j % 4
        dz = 4 + (k % 2) * ((k + 1) // 2) - (1 - k % 2) * (k // 2)
        dy = 2 + (i % 2) * ((i + 1) // 2) - (1 - i % 2) * (i // 2)
        return (self.z + dz) % 8, (self.y + dy) % 4

    def is_me(self, z, y, core):
        return (z == self.z) & (y == self.y) & (core == self.core)


def greet(me):
    barrier = pltpu.get_barrier_semaphore()

    def one(i):
        z, y = me.far(i // 2)
        core = i % 2

        @pl.when(jnp.logical_not(me.is_me(z, y, core)))
        def _():
            pl.semaphore_signal(barrier, 1, device_id=me.at(z, y, core), device_id_type=MESH)

    def other(i):
        here = i == 4
        z = jnp.where(here, me.z, i % 4 + 4 * (me.z // 4))
        core = jnp.where(here, 1 - me.core, me.core)
        pl.semaphore_signal(barrier, 1, device_id=me.at(z, me.y, core, 1 - me.plane), device_id_type=MESH)

    loop(64, one)
    loop(5, other)
    return barrier


def send(src, dst, send_sem, recv_sem, device):
    return pltpu.make_async_remote_copy(
        src_ref=src, dst_ref=dst, send_sem=send_sem, recv_sem=recv_sem, device_id=device, device_id_type=MESH
    )


def arrived(ref, sem):
    pltpu.make_async_copy(ref, ref, sem).wait()


def start_either(here, remote, local):
    @pl.when(here)
    def _():
        local.start()

    @pl.when(jnp.logical_not(here))
    def _():
        remote.start()


def end_either(here, remote, local):
    @pl.when(jnp.logical_not(here))
    def _():
        remote.wait_send()


def kernel(
    doc_ref, source_ref, q_ref, k_ref, v_ref, lat_ref, gain_ref,
    att_ref, emb_ref,
    q_in, qs, qp, kv, lat_in, gain_in, ka, va, qa, o_ref, res,
    home, sq_out, sq_in, doc_out, doc_in, norm_out, norm_in, row_out, row_in,
    s_a, r_a, s_b, r_b, s_c, r_c, s_s, r_s, s_q, r_q, s_l, r_l, l_q,
    s_o, r_o, s_sq, r_sq, s_d, r_d, s_n, r_n, s_e, r_e,
    att, l_att,
):
    me = Place()
    z, y, core = me.z, me.y, me.core
    load_q = pltpu.make_async_copy(q_ref, q_in, l_q)
    load_q.start()
    barrier = greet(me)

    load_q.wait()

    def regroup(i):
        half, pair = i // 8, i % 8
        rows_at = pl.ds(pl.multiple_of(pair * 16, 16), 16)
        for block in range(2):
            tile = q_in[block, rows_at, pl.ds(pl.multiple_of(half * 512, 512), 512)].astype(F32)
            for part in range(2):
                rows = tile[part * 8 : part * 8 + 8]
                rows = jnp.concatenate([rows[:, h * 128 : h * 128 + 128] for h in range(4)], axis=0)
                qs[2 * i + part, block * ROWS : block * ROWS + ROWS, :] = rows.astype(BF16)

    loop(16, regroup)
    va[:, :, 128:256] = jnp.ones((BLOCKS, BLOCK, 128), BF16)

    first = jnp.int32(0)
    for i in range(BLOCKS - LONG + 1):
        first = jnp.where(doc_ref[i] == doc_ref[i + LONG - 1], i, first)

    def packed(i):
        i = jnp.int32(i)
        return jnp.where(i < LONG, first + i, jnp.where(i - LONG < first, i - LONG, i))

    def sorted_place(at):
        return jnp.where(at < first, at + LONG, jnp.where(at < first + LONG, at - first, at))

    pl.semaphore_wait(barrier, 68)

    up, down = (y + 1) % 4, (y + 3) % 4
    mine = me.kv // 2 == core

    def order(j):
        odd = j % 2
        return odd * ((j + 1) // 2) + (1 - odd) * (8 - j // 2)

    def column(j, run):
        to_z = (z + order(j)) % 8

        @pl.when((to_z % 4) // 2 == core)
        def _():
            half = to_z % 2
            for part in range(PARTS):
                for kind in range(2):
                    first = part * PART
                    columns = pl.ds(pl.multiple_of(half * HEAD_DIM, HEAD_DIM), HEAD_DIM)
                    src = (k_ref, v_ref)[kind].at[pl.ds(first, PART), columns]
                    dst = kv.at[kind, pl.ds(pl.multiple_of(me.ctx * 256 + first, PART), PART), :]
                    sem = r_a.at[part, z]
                    here = (to_z == z) & (core == kind)
                    copy = send(src, dst, s_a.at[part, kind, to_z], sem, me.at(to_z, y, kind))
                    run(here, copy, pltpu.make_async_copy(src, dst, sem))

    loop(AHEAD, lambda j: column(j, start_either))

    def query(j, run):
        i = (j + me.ctx) % 32
        to = me.worker(2 * core + i // 16, i % 16)
        run(
            me.is_me(*to),
            send(qs.at[i], qp.at[me.ctx], s_q.at[i], r_q.at[me.ctx], me.at(*to)),
            pltpu.make_async_copy(qs.at[i], qp.at[me.ctx], r_q.at[me.ctx]),
        )

    def rows_of(from_z, from_y, first=0, count=256):
        start = pl.multiple_of((from_z * 4 + from_y) * 256 + first, HALF)
        return kv.at[core, pl.ds(start, count), :]

    def to_core(from_z):
        rows = kv.at[core, pl.ds(pl.multiple_of(from_z * 1024, 1024), 1024), :]
        return send(rows, rows, s_s.at[from_z], r_s.at[from_z], me.at(z, y, 1 - core))

    def near(from_z, part):
        rows = rows_of(from_z, y, part * PART, PART)
        return (
            send(rows, rows, s_b.at[0, part, from_z], r_b.at[0, part, from_z], me.at(z, up, core)),
            send(rows, rows, s_b.at[1, part, from_z], r_b.at[1, part, from_z], me.at(z, down, core)),
        )

    def onward(from_z, part):
        one = rows_of(from_z, down, part * PART, HALF)
        two = rows_of(from_z, up, part * PART + HALF, HALF)
        return (
            send(one, one, s_c.at[0, part, from_z], r_c.at[0, part, from_z], me.at(z, up, core)),
            send(two, two, s_c.at[1, part, from_z], r_c.at[1, part, from_z], me.at(z, down, core)),
        )

    steps = 8 * PARTS

    def at_step(e):
        return (z + order(e // PARTS)) % 8, e % PARTS

    def arrange_keys(j):
        from_z = (z + order(j)) % 8
        rows = pl.ds(pl.multiple_of(from_z * 1024, 1024), 1024)
        blocks = pl.ds(from_z * 8, 8)
        arrived(kv.at[1 - core, rows, :], r_s.at[from_z])
        key = kv[0, rows, :].reshape(8, BLOCK, 128)
        ka[blocks, :, 0:128] = key
        ka[blocks, :, 128:256] = key
        va[blocks, :, 0:128] = kv[1, rows, :].reshape(8, BLOCK, 128)

    def ring(e):
        @pl.when(e < steps)
        def _():
            @pl.when((e % PARTS == 0) & (e // PARTS + AHEAD < 8))
            def _():
                column(e // PARTS + AHEAD, start_either)

            from_z, part = at_step(e)
            arrived(rows_of(from_z, y, part * PART, PART), r_a.at[part, from_z])
            for copy in near(from_z, part):
                copy.start()

        @pl.when((e >= Q_START) & (e < Q_START + 32 // Q_STEP))
        def _():
            for i in range(Q_STEP):
                query((e - Q_START) * Q_STEP + i, start_either)

        @pl.when((e >= LAG) & (e < steps + LAG))
        def _():
            from_z, part = at_step(e - LAG)
            copies = onward(from_z, part)
            arrived(rows_of(from_z, down, part * PART, PART), r_b.at[0, part, from_z])
            copies[0].start()
            arrived(rows_of(from_z, up, part * PART, PART), r_b.at[1, part, from_z])
            copies[1].start()

        @pl.when(e >= 2 * LAG)
        def _():
            from_z, part = at_step(e - 2 * LAG)
            opposite = (y + 2) % 4
            arrived(rows_of(from_z, opposite, part * PART, HALF), r_c.at[0, part, from_z])
            arrived(rows_of(from_z, opposite, part * PART + HALF, HALF), r_c.at[1, part, from_z])

            @pl.when(part == PARTS - 1)
            def _():
                to_core(from_z).start()

        @pl.when(e >= 2 * LAG + LAY)
        def _():
            arrange_keys(e - 2 * LAG - LAY)

    def pool_inputs():
        other = me.at(z, y, 1 - core)
        half = me.kv % 2
        lat = lat_ref.at[:, pl.ds(pl.multiple_of(half * 512, 512), 512)]
        gain = gain_ref.at[half]
        return (
            pltpu.make_async_copy(lat, lat_in, r_l.at[0]),
            pltpu.make_async_copy(gain, gain_in, r_l.at[1]),
            send(lat, lat_in, s_l.at[0], r_l.at[0], other),
            send(gain, gain_in, s_l.at[1], r_l.at[1], other),
        )

    @pl.when(mine)
    def _():
        for copy in pool_inputs():
            copy.start()

    loop(steps + 2 * LAG, ring)


    def sends_done():
        loop(8, lambda j: column(j, end_either))

        def ring_done(e):
            from_z, part = at_step(e)
            for copy in near(from_z, part) + onward(from_z, part):
                copy.wait_send()

        loop(steps, ring_done)
        loop(32, lambda j: query(j, end_either))
        loop(8, lambda from_z: to_core(from_z).wait_send())

        @pl.when(mine)
        def _():
            for copy in pool_inputs()[2:]:
                copy.wait_send()

    scale = math.log2(math.e) * HEAD_DIM ** (-0.5)

    def arrange_queries(s):
        arrived(qp.at[s], r_q.at[s])
        query = qp[s].reshape(2, ROWS, 128).astype(F32) * scale
        high = query.astype(BF16)
        blocks = pl.ds(2 * s, 2)
        qa[blocks, :, 0:128] = high
        qa[blocks, :, 128:256] = (query - high.astype(F32)).astype(BF16)

    loop(32, arrange_queries)
    loop(LAY, lambda j: arrange_keys(8 - LAY + j))

    for copy in pool_inputs()[:2]:
        copy.wait()

    def blocks_of(ref, first_block, count):
        return jnp.concatenate([ref[packed(first_block + b)] for b in range(count)], axis=0)

    def attend_rows(q, keys_at, chunks, rows, docs=None):
        m = total = None
        for c in range(chunks):
            key, value, key_docs = keys_at(c)
            s = lax.dot_general(q, key, (((1,), (1,)), ((), ())), preferred_element_type=F32)
            parts = [s[:, b * 128 : b * 128 + 128] for b in range(CHUNK // 128)]
            if docs is not None:
                parts = [jnp.where(docs == doc, part, -1e30) for doc, part in zip(key_docs, parts)]
            top = functools.reduce(jnp.maximum, parts)
            top = jnp.broadcast_to(jnp.max(top, axis=1, keepdims=True), top.shape)
            new_m = top if m is None else jnp.maximum(m, top)
            w = jnp.concatenate([jnp.exp2(part - new_m).astype(BF16) for part in parts], axis=1)
            add = jnp.dot(w, value, preferred_element_type=F32)
            if m is None:
                total = add
            else:
                shrink = jnp.exp2(m - new_m)
                total = total * jnp.concatenate([shrink, shrink], axis=1) + add
            m = new_m
        o_ref[rows] = (total[:, 0:128] / total[:, 128:256]).astype(BF16).reshape(-1, ROWS, 128)

    per_chunk = CHUNK // BLOCK

    def long_keys(c):
        return blocks_of(ka, c * per_chunk, per_chunk), blocks_of(va, c * per_chunk, per_chunk), None

    def long_tile(t):
        per = TILE // ROWS
        attend_rows(blocks_of(qa, t * per, per), long_keys, LONG_KEYS // CHUNK, pl.ds(t * per, per))

    reach = BLOCKS - LONG - DOCS + 1
    per_short = SHORT_TILE // ROWS

    def short_keys(first_chunk):
        def keys(c):
            at = LONG + (first_chunk + c) * per_chunk
            docs = [doc_ref[packed(at + b)] for b in range(per_chunk)]
            return blocks_of(ka, at, per_chunk), blocks_of(va, at, per_chunk), docs

        return keys

    def short_tile(t):
        at = LONG + t * per_short
        low = max(0, t * per_short - reach) // per_chunk
        high = -(-min(BLOCKS - LONG, (t + 1) * per_short + reach) // per_chunk)
        docs = jnp.concatenate(
            [jnp.full((ROWS, 128), doc_ref[packed(at + b)], jnp.int32) for b in range(per_short)], axis=0
        )
        attend_rows(blocks_of(qa, at, per_short), short_keys(low), high - low, pl.ds(at, per_short), docs)

    for t in range((BLOCKS - LONG) // per_short):
        short_tile(t)
    loop(LONG * ROWS // TILE, long_tile)

    whole = o_ref[...].astype(F32).reshape(BLOCKS, 4, PIECE, 128)
    square = jnp.sum(whole * whole, axis=1).reshape(BLOCKS * PIECE, 128)
    high = square.astype(BF16)
    low = (square - high.astype(F32)).astype(BF16)
    ones = jnp.ones((8, 128), BF16)
    dims = (((1,), (1,)), ((), ()))
    sq_out[...] = lax.dot_general(ones, high, dims, preferred_element_type=F32) + lax.dot_general(
        ones, low, dims, preferred_element_type=F32
    )

    me8 = me.plane * 4 + me.kv
    home_core = me.kv // 2
    half = me.kv % 2

    def partners(src, box, s_sem, r_sem, run):
        def one(i):
            @pl.when(i != me8)
            def _():
                device = me.at(i % 4 + 4 * (me.z // 4), me.y, me.core, i // 4)
                run(send(src, box.at[me8], s_sem.at[i], r_sem.at[me8], device))

        loop(8, one)

    def from_partners(box, r_sem):
        def one(i):
            @pl.when(i != me8)
            def _():
                arrived(box.at[i], r_sem.at[i])

        loop(8, one)

    start = lambda copy: copy.start()
    sent = lambda copy: copy.wait_send()

    partners(sq_out, sq_in, s_sq, r_sq, start)
    sq_in[me8] = sq_out[...]

    def result(j, run):
        s = (j + me.ctx) % 32
        src = res.at[pl.ds(2 * s, 2)]
        slot = half * 16 + me.piece
        run(
            me.is_me(s // 4, s % 4, home_core),
            send(src, home.at[slot], s_o.at[s], r_o.at[slot], me.at(s // 4, s % 4, home_core)),
            pltpu.make_async_copy(src, home.at[slot], r_o.at[slot]),
        )

    def move(p):
        res[p] = o_ref[sorted_place(source_ref[p])]

    loop(BLOCKS, move)
    loop(32, lambda j: result(j, start_either))

    lat = lat_in[...]
    gained = []
    for h in range(4):
        part = whole[:, h].reshape(BLOCKS * PIECE, 128)
        gained.append((part * gain_in[h : h + 1, :]).astype(BF16))
    gained = jnp.concatenate(gained, axis=1)
    s = lax.dot_general(lat, gained, (((1,), (1,)), ((), ())), preferred_element_type=F32)
    tokens = lax.broadcasted_iota(jnp.int32, (DOCS, PIECE), 0)
    hot = jnp.concatenate(
        [(tokens == doc_ref[packed(i)]).astype(F32) for i in range(BLOCKS)], axis=1
    ).astype(BF16)
    from_partners(sq_in, r_sq)
    channel_total = jnp.sum(sq_in[...], axis=0)
    factor = lax.rsqrt(channel_total / CHANNELS + EPS) * (math.log2(math.e) * 512 ** (-0.5))
    s = s.reshape(64, 8, BLOCKS * PIECE) * factor[None]
    top = jnp.max(jnp.max(s, axis=0), axis=0, keepdims=True)
    w = jnp.exp2(s - top[None])
    w = w * (1.0 / jnp.sum(jnp.sum(w, axis=0), axis=0, keepdims=True))[None]
    w = w.reshape(512, BLOCKS * PIECE).astype(BF16)
    by_doc = lax.dot_general(hot, w, (((1,), (1,)), ((), ())), preferred_element_type=F32)
    sums = None
    for _ in range(3):
        part = by_doc.astype(BF16)
        by_doc = by_doc - part.astype(F32)
        add = jnp.dot(part, lat, preferred_element_type=F32)
        sums = add if sums is None else sums + add

    w8 = me.piece % 8
    doc_out[...] = jnp.concatenate(
        [
            sums[two * 8 : two * 8 + 8, h * 128 : h * 128 + 128].reshape(8, 1, 128)
            for two in range(2)
            for h in range(4)
        ],
        axis=1,
    )

    def document(w, run):
        run(
            w == w8,
            send(doc_out.at[w], doc_in.at[w8], s_d.at[w], r_d.at[w8], me.at(me.z, w // 2, w % 2)),
            pltpu.make_async_copy(doc_out.at[w], doc_in.at[w8], r_d.at[w8]),
        )

    loop(8, lambda w: document(w, start_either))
    loop(8, lambda w: arrived(doc_in.at[w], r_d.at[w]))
    row_out[...] = jnp.sum(doc_in[...], axis=0)

    def share(j, run):
        to_z, to_y = me.far(j)
        dst = row_in.at[half, me.piece]
        slot = half * 16 + me.piece
        run(
            me.is_me(to_z, to_y, home_core),
            send(row_out, dst, s_e.at[j], r_e.at[slot], me.at(to_z, to_y, home_core)),
            pltpu.make_async_copy(row_out, dst, r_e.at[slot]),
        )

    loop(32, lambda j: share(j, start_either))
    sends_done()

    loop(32, lambda i: arrived(home.at[i], r_o.at[i]))
    for side in range(2):
        for block in range(2):
            for pair in range(8):
                rows = []
                for part in range(2):
                    piece = home[side * 16 + pair * 2 + part, block].astype(F32)
                    rows.append(jnp.concatenate([piece[h * 8 : h * 8 + 8] for h in range(4)], axis=1))
                at = block * BLOCK + pair * 16
                att[at : at + 16, side * 512 : side * 512 + 512] = jnp.concatenate(rows, axis=0).astype(BF16)
    att_out = pltpu.make_async_copy(att, att_ref, l_att)
    att_out.start()

    loop(32, lambda i: arrived(row_in.at[i // 16, i % 16], r_e.at[i]))
    rows = row_in[...]
    rows = rows[:, 0:8] + rows[:, 8:16]
    for two in range(2):
        square = rows[:, :, two * 4 : two * 4 + 4, :]
        square = jnp.sum(square * square, axis=(0, 2))
        norm_out[two] = jnp.broadcast_to(jnp.sum(square, axis=-1, keepdims=True), (8, 128))
    my_head = me.plane * 2 + core

    def head(i, run):
        @pl.when(i != my_head)
        def _():
            device = me.at(me.z, me.y, i % 2, i // 2)
            run(send(norm_out, norm_in.at[my_head], s_n.at[i], r_n.at[my_head], device))

    loop(4, lambda i: head(i, start))
    norm_in[my_head] = norm_out[...]

    def from_head(i):
        @pl.when(i != my_head)
        def _():
            arrived(norm_in.at[i], r_n.at[i])

    partners(sq_out, sq_in, s_sq, r_sq, sent)
    loop(32, lambda j: result(j, end_either))
    loop(8, lambda w: document(w, end_either))
    loop(32, lambda j: share(j, end_either))
    loop(4, lambda i: head(i, sent))
    loop(4, from_head)
    factors = lax.rsqrt(jnp.sum(norm_in[...], axis=0) / CHANNELS + EPS)
    for side in range(2):
        for h in range(4):
            at = side * 512 + h * 128
            for two in range(2):
                emb_ref[two * 8 : two * 8 + 8, at : at + 128] = rows[side, :, two * 4 + h, :] * factors[two]
    att_out.wait()


def shards(queries, keys, values, latents, norm_gain, block_doc, block_source):
    dma = pltpu.SemaphoreType.DMA
    hbm = pl.BlockSpec(memory_space=pltpu.HBM)
    vmem = pl.BlockSpec(memory_space=pltpu.VMEM)
    smem = pl.BlockSpec(memory_space=pltpu.SMEM)
    tokens = BLOCKS * BLOCK
    outs = pl.pallas_call(
        kernel,
        out_shape=(
            jax.ShapeDtypeStruct((256, 1024), BF16),
            jax.ShapeDtypeStruct((DOCS, 1024), F32),
        ),
        in_specs=[smem, smem] + [hbm] * 5,
        out_specs=(hbm, vmem),
        scratch_shapes=[
            pltpu.VMEM((2, BLOCK, 1024), BF16),
            pltpu.VMEM((32, 2 * ROWS, HEAD_DIM), BF16),
            pltpu.VMEM((32, 2 * ROWS, HEAD_DIM), BF16),
            pltpu.VMEM((2, tokens, HEAD_DIM), BF16),
            pltpu.VMEM((512, 512), BF16),
            pltpu.VMEM((4, 128), F32),
            pltpu.VMEM((BLOCKS, BLOCK, 256), BF16),
            pltpu.VMEM((BLOCKS, BLOCK, 256), BF16),
            pltpu.VMEM((BLOCKS, ROWS, 256), BF16),
            pltpu.VMEM((BLOCKS, ROWS, HEAD_DIM), BF16),
            pltpu.VMEM((BLOCKS, ROWS, HEAD_DIM), BF16),
            pltpu.VMEM((32, 2, ROWS, HEAD_DIM), BF16),
            pltpu.VMEM((8, BLOCKS * PIECE), F32),
            pltpu.VMEM((8, 8, BLOCKS * PIECE), F32),
            pltpu.VMEM((8, 8, 128), F32),
            pltpu.VMEM((8, 8, 128), F32),
            pltpu.VMEM((2, 8, 128), F32),
            pltpu.VMEM((4, 2, 8, 128), F32),
            pltpu.VMEM((8, 128), F32),
            pltpu.VMEM((2, 16, 8, 128), F32),
            dma((PARTS, 2, 8)), dma((PARTS, 8)),
            dma((2, PARTS, 8)), dma((2, PARTS, 8)),
            dma((2, PARTS, 8)), dma((2, PARTS, 8)),
            dma((8,)), dma((8,)),
            dma((32,)), dma((32,)),
            dma((2,)), dma((2,)),
            dma,
            dma((32,)), dma((32,)),
            dma((8,)), dma((8,)),
            dma((8,)), dma((8,)),
            dma((4,)), dma((4,)),
            dma((32,)), dma((32,)),
            pltpu.VMEM((256, 1024), BF16),
            dma,
        ],
        compiler_params=pltpu.CompilerParams(
            collective_id=0, has_side_effects=True, vmem_limit_bytes=60 * 1024 * 1024
        ),
        name="embed",
    )(
        block_doc, block_source, queries.reshape(2, BLOCK, 1024), keys, values, latents, norm_gain.reshape(2, 4, 128)
    )
    return written(*outs)


def out_kernel(att_ref, emb_ref, att_out, emb_out, att, emb, sems_in, sems_out):
    pieces = [(emb_ref, emb, emb_out)]
    for i in range(4):
        rows = pl.ds(64 * i, 64)
        pieces.append((att_ref.at[rows], att.at[rows], att_out.at[rows]))
    into = [pltpu.make_async_copy(src, held, sems_in.at[i]) for i, (src, held, _) in enumerate(pieces)]
    out = [pltpu.make_async_copy(held, dst, sems_out.at[i]) for i, (_, held, dst) in enumerate(pieces)]
    for copy in into:
        copy.start()
    for one, two in zip(into, out):
        one.wait()
        two.start()
    for copy in out:
        copy.wait()


def written(attended, embeddings):
    hbm = pl.BlockSpec(memory_space=pltpu.HBM)
    return pl.pallas_call(
        out_kernel,
        out_shape=(
            jax.ShapeDtypeStruct(attended.shape, attended.dtype),
            jax.ShapeDtypeStruct(embeddings.shape, embeddings.dtype),
        ),
        in_specs=[hbm, hbm],
        out_specs=(hbm, hbm),
        scratch_shapes=[
            pltpu.VMEM(attended.shape, attended.dtype),
            pltpu.VMEM(embeddings.shape, embeddings.dtype),
            pltpu.SemaphoreType.DMA((5,)),
            pltpu.SemaphoreType.DMA((5,)),
        ],
        compiler_params=pltpu.CompilerParams(vmem_limit_bytes=60 * 1024 * 1024),
        name="written",
    )(attended, embeddings)


def solution(mesh):
    in_specs = (
        P(("dp", "ctx"), "head"),
        P(("dp", "ctx"), "head"),
        P(("dp", "ctx"), "head"),
        P(None, "head"),
        P("head"),
        P("dp"),
        P("dp"),
    )
    out_specs = (P(("dp", "ctx"), "head"), P("dp", "head"))
    return jax.shard_map(shards, mesh=mesh, in_specs=in_specs, out_specs=out_specs, check_vma=False)
```
